32 devices in a mesh: tgt: 32 (over z, y, x, core), src: 1.
Axes of the slice: x: 2, y: 2, z: 4, core: 2. Of those that a mesh axis runs over, the one named last changes fastest.
Arguments:
- connectome: bfloat16 [4096, 51200], P('tgt', 'src'), may hold values from -0.02734375 to 0.02734375
- history: bfloat16 [32, 32, 51200], P('tgt', None, 'src'), may hold values from 0 to 5
- delays: int32 [32, 400], P('tgt', 'src'), may hold values from 16 to 32
- cycle_head: int32 [1], replicated, may hold values from 0 to 31
- outside_afferent: float32 [32], replicated, may hold values from 120 to 320
- init_state: float32 [6, 32, 4096], P(None, None, 'tgt'), may hold values from -4 to 4
- lead_field: bfloat16 [4096, 256], P('tgt'), may hold values from -0.09375 to 0.09375
Outputs:
- sensor_signal: float32 [32, 16, 256], P('tgt')
- final_state: float32 [6, 32, 4096], P(None, None, ('tgt', 'src'))
The draws below stay inside these ranges and needn't reach their ends.
Inputs may be any that keep to these rules, and one draw needn't show every extreme that they name: `cycle_head`: a slot of the history cycle.
All inputs are finite; a program needn't handle non-finite values.
Results may differ from the reference program's by a relative error of at most 0.003.
Values may be sent and summed in bfloat16 or wider, within the bound.
A program may use at most 320 MiB of HBM per device.

```python
import math
import jax
import jax.numpy as jnp
from jax import lax

V = 51200
SENSORS = 256
MEM = 32
STEPS = 16
HIST = 32
SB = 128
TB = 128
TARGETS = 4096


def place_ends(result, own_key, smallest, high):
    index_at = [jax.random.randint(jax.random.fold_in(own_key, axis), (), 0, length) for axis, length in enumerate(result.shape)]
    widest = result.shape.index(max(result.shape))
    next_to = index_at[:widest] + [(index_at[widest] + 1) % result.shape[widest]] + index_at[widest + 1:]
    return result.at[tuple(index_at)].set(smallest).at[tuple(next_to)].set(high)


def levels(own_key, shape, split, smallest, top_value):
    gain = 1.0
    for axis_at, parts in split:
        heights = jax.random.uniform(jax.random.fold_in(jax.random.fold_in(own_key, 6), axis_at), (parts,), jnp.float32, smallest / len(split), top_value / len(split))
        gain = gain * jnp.repeat(jnp.exp(heights), shape[axis_at] // parts).reshape((-1,) + (1,) * (len(shape) - 1 - axis_at))
    return gain


def normal_values(stream_key, dims, spread, most, shards=(), kind=jnp.bfloat16):
    level = levels(stream_key, dims, shards, -0.22, 0.18) if shards else 1.0
    array = jax.random.normal(stream_key, dims, jnp.float32) * spread * level
    return jnp.minimum(jnp.maximum(array, -most), most).astype(kind)


def setup_inputs(seed: int = 0) -> dict:
    arg_keys = jax.random.split(jax.random.key(seed), 8)
    return {
        "connectome": normal_values(arg_keys[0], (TARGETS, V), V ** -0.5, 0.02734375, ((0, 32),)),
        "history": jnp.clip(5.0 * jax.random.uniform(arg_keys[1], (HIST, MEM, V), jnp.float32) ** levels(arg_keys[1], (HIST, MEM, V), ((0, 32),), -0.2, 0.2), 0.0, 5.0).astype(jnp.bfloat16),
        "delays": place_ends(jax.random.randint(arg_keys[2], (TARGETS // TB, V // SB), STEPS, HIST + 1), jax.random.fold_in(arg_keys[2], 1), STEPS, HIST).astype(jnp.int32),
        "cycle_head": jax.random.randint(arg_keys[3], (1,), 0, HIST).astype(jnp.int32),
        "outside_afferent": jnp.clip(jnp.exp(jax.random.uniform(arg_keys[4], (MEM,), jnp.float32, math.log(120.0), math.log(320.0))), 120.0, 320.0),
        "init_state": normal_values(arg_keys[5], (6, MEM, TARGETS), 1.0, 4.0, ((2, 32),), jnp.float32),
        "lead_field": normal_values(arg_keys[6], (TARGETS, SENSORS), TARGETS ** -0.5, 0.09375, ((0, 32),)),
    }


integrator_step_width = 0.1
positive_synaptic_amplitude = 0.0325
negative_synaptic_amplitude = 0.11
interneuron_fraction = 0.5
global_link_scale = 30.0
stellate_contact_count = 135.0
recurrent_loop_contacts = 108.0
interneuron_contact_count = 33.75
peak_spike_rate = 5.0
logistic_slope_factor = 0.56
logistic_midpoint = 6.0


def spike_rate_response(cell_depolarization):
    return peak_spike_rate * jax.nn.sigmoid(logistic_slope_factor * (cell_depolarization - logistic_midpoint))


def advance(carry, applied_stimulus, outside_afferent):
    principal_cell_depolarization, stellate_mean_depolarization, interneuron_mean_depolarization, principal_cell_slope, excite_rate, interneuron_slope = carry
    next_principal_cell_slope = principal_cell_slope + integrator_step_width * (positive_synaptic_amplitude * spike_rate_response(stellate_mean_depolarization - interneuron_mean_depolarization) - 2.0 * principal_cell_slope - principal_cell_depolarization)
    summed_afferent_rate = outside_afferent[:, None] + recurrent_loop_contacts * spike_rate_response(stellate_contact_count * principal_cell_depolarization) + global_link_scale * applied_stimulus
    new_excite_rate = excite_rate + integrator_step_width * (positive_synaptic_amplitude * summed_afferent_rate - 2.0 * excite_rate - stellate_mean_depolarization)
    next_interneuron_slope = interneuron_slope + integrator_step_width * (negative_synaptic_amplitude * interneuron_contact_count * spike_rate_response(interneuron_contact_count * principal_cell_depolarization) - 2.0 * interneuron_fraction * interneuron_slope - interneuron_fraction * interneuron_fraction * interneuron_mean_depolarization)
    return (principal_cell_depolarization + integrator_step_width * principal_cell_slope, stellate_mean_depolarization + integrator_step_width * excite_rate, interneuron_mean_depolarization + integrator_step_width * interneuron_slope, next_principal_cell_slope, new_excite_rate, next_interneuron_slope)


def integrate(init_state, outside_afferent, coupling):
    def one_step(carry, applied_stimulus):
        fresh = advance(carry, applied_stimulus, outside_afferent)
        return fresh, fresh[1] - fresh[2]

    begin = tuple(init_state[member] for member in range(6))
    final, potentials = lax.scan(one_step, begin, coupling)
    return jnp.stack(final), potentials


def reference(connectome, history, delays, cycle_head, outside_afferent, init_state, lead_field):
    tiles = connectome.reshape(TARGETS // TB, TB, V // SB, SB)
    stacked = history.astype(jnp.float32).reshape(HIST, MEM, V // SB, SB)
    moments = jnp.arange(STEPS, dtype=jnp.int32)
    slot_ids = jnp.arange(HIST, dtype=jnp.int32)

    def one_block(pair):
        tile, lags = pair
        lag_slot = (cycle_head[0] + moments[:, None] - lags[None, :]) % HIST
        picker = (lag_slot[:, None, :] == slot_ids[None, :, None]).astype(jnp.float32)
        window = jnp.einsum("tkb,kmbs->tmbs", picker, stacked, precision=lax.Precision.HIGHEST)
        window = lax.optimization_barrier(window.astype(jnp.bfloat16)).astype(jnp.float32)
        return jnp.einsum("rbs,tmbs->tmr", tile.astype(jnp.float32), window, precision=lax.Precision.HIGHEST)

    blocks_out = lax.map(one_block, (tiles, delays))
    coupling = jnp.transpose(blocks_out, (1, 2, 0, 3)).reshape(STEPS, MEM, TARGETS)
    final_state, potentials = integrate(init_state, outside_afferent, coupling)
    potential = lax.optimization_barrier(potentials.astype(jnp.bfloat16)).astype(jnp.float32)
    signal = jnp.einsum("tmr,rs->mts", potential, lead_field.astype(jnp.float32), precision=lax.Precision.HIGHEST)
    return signal, final_state
```

```python
import functools

import jax
import jax.numpy as jnp
from jax import lax
from jax.experimental import pallas as pl
from jax.experimental.pallas import tpu as pltpu
from jax.sharding import PartitionSpec as P

STEPS = 16
MESH = pl.DeviceIdType.MESH
GROUP = 8
CHUNKS = 5


integrator_step_width = 0.1
positive_synaptic_amplitude = 0.0325
negative_synaptic_amplitude = 0.11
interneuron_fraction = 0.5
global_link_scale = 30.0
stellate_contact_count = 135.0
recurrent_loop_contacts = 108.0
interneuron_contact_count = 33.75
peak_spike_rate = 5.0
logistic_slope_factor = 0.56
logistic_midpoint = 6.0


def spike_rate_response(cell_depolarization):
    return peak_spike_rate * jax.nn.sigmoid(
        logistic_slope_factor * (cell_depolarization - logistic_midpoint)
    )


def advance(carry, applied_stimulus, outside_afferent):
    (
        principal_cell_depolarization,
        stellate_mean_depolarization,
        interneuron_mean_depolarization,
        principal_cell_slope,
        excite_rate,
        interneuron_slope,
    ) = carry
    next_principal_cell_slope = principal_cell_slope + integrator_step_width * (
        positive_synaptic_amplitude
        * spike_rate_response(stellate_mean_depolarization - interneuron_mean_depolarization)
        - 2.0 * principal_cell_slope
        - principal_cell_depolarization
    )
    summed_afferent_rate = (
        outside_afferent
        + recurrent_loop_contacts
        * spike_rate_response(stellate_contact_count * principal_cell_depolarization)
        + global_link_scale * applied_stimulus
    )
    new_excite_rate = excite_rate + integrator_step_width * (
        positive_synaptic_amplitude * summed_afferent_rate
        - 2.0 * excite_rate
        - stellate_mean_depolarization
    )
    next_interneuron_slope = interneuron_slope + integrator_step_width * (
        negative_synaptic_amplitude
        * interneuron_contact_count
        * spike_rate_response(interneuron_contact_count * principal_cell_depolarization)
        - 2.0 * interneuron_fraction * interneuron_slope
        - interneuron_fraction * interneuron_fraction * interneuron_mean_depolarization
    )
    return (
        principal_cell_depolarization + integrator_step_width * principal_cell_slope,
        stellate_mean_depolarization + integrator_step_width * excite_rate,
        interneuron_mean_depolarization + integrator_step_width * interneuron_slope,
        next_principal_cell_slope,
        new_excite_rate,
        next_interneuron_slope,
    )


def integrate(init_state, outside_afferent, coupling):

    def one_step(carry, applied_stimulus):
        fresh = advance(carry, applied_stimulus, outside_afferent[:, None])
        return (fresh, fresh[1] - fresh[2])

    begin = tuple((init_state[member] for member in range(6)))
    final, potentials = lax.scan(one_step, begin, coupling)
    return (jnp.stack(final), potentials)


def body(connectome, history, delays, cycle_head, outside_afferent, init_state, lead_field):
    tgt_rows = connectome.shape[0]
    target_blocks = delays.shape[0]
    source_blocks = delays.shape[1]
    block_rows = tgt_rows // target_blocks
    block_cols = connectome.shape[1] // source_blocks
    members = history.shape[1]
    slots_all = history.shape[0] * lax.axis_size("tgt")
    tiles = connectome.reshape(target_blocks, block_rows, source_blocks, block_cols)
    moments = jnp.arange(STEPS, dtype=jnp.int32)
    lag_slot = (cycle_head[0] + moments[None, None, :] - delays[:, :, None]) % slots_all
    whole = lax.all_gather(history, "tgt", axis=0, tiled=True)
    stacked = whole.reshape(slots_all, members, source_blocks, block_cols)
    slot_ids = jnp.arange(slots_all, dtype=jnp.int32)
    wanted = lag_slot[0].T
    picker = (wanted[:, None, :] == slot_ids[None, :, None]).astype(jnp.bfloat16)
    window = jnp.einsum(
        "tkb,kmbs->tmbs", picker, stacked, preferred_element_type=jnp.float32
    ).astype(jnp.bfloat16)
    pieces = jnp.einsum("rbs,tmbs->tmr", tiles[0], window, preferred_element_type=jnp.float32)
    share = tgt_rows // lax.axis_size("src")
    offset_rows = lax.axis_index("src") * share
    summed = lax.psum(pieces, "src")
    final_full, potentials = integrate(init_state, outside_afferent, summed)
    final_state = lax.dynamic_slice_in_dim(final_full, offset_rows, share, 2)
    potential = potentials.astype(jnp.bfloat16)
    signal = lax.psum_scatter(
        jnp.einsum("tmr,rs->mts", potential, lead_field, preferred_element_type=jnp.float32),
        "tgt",
        scatter_dimension=0,
        tiled=True,
    )
    return (signal, final_state)


def fused_kernel(
    planes,
    conn_ref,
    hist_ref,
    delay_ref,
    head_ref,
    outside_ref,
    init_ref,
    lead_ref,
    signal_ref,
    final_ref,
    *scratch,
):
    held = scratch[:CHUNKS]
    tiles = scratch[CHUNKS : 2 * CHUNKS]
    (
        delay_vmem,
        delay_smem,
        acc,
        parts,
        pot,
        eeg,
        eeg_plane,
        eeg_sum,
        eeg_line,
        piece_send,
        piece_recv,
        up_send,
        up_recv,
        down_send,
        down_recv,
        tile_send,
        tile_recv,
        delay_send,
        delay_recv,
        delay_local,
        part_send,
        part_recv,
        plane_send,
        plane_recv,
        line_send,
        line_recv,
    ) = scratch[2 * CHUNKS :]
    me = lax.axis_index("tgt")
    z = me // GROUP
    p = me % GROUP
    rows = conn_ref.shape[0]
    members = hist_ref.shape[1]
    share = conn_ref.shape[1] // GROUP
    width = share // CHUNKS
    blocks = delay_ref.shape[1] // GROUP
    chunk_blocks = blocks // CHUNKS
    block_cols = width // chunk_blocks

    def peer(off):
        return lax.rem(p + off, GROUP)

    def line(off):
        return lax.rem(z + off, planes)

    def device(plane, place):
        return {"tgt": plane * GROUP + place}

    barrier = pltpu.get_barrier_semaphore()
    for off in range(1, GROUP):
        pl.semaphore_signal(barrier, inc=1, device_id=device(z, peer(off)), device_id_type=MESH)
    for off in range(1, planes):
        pl.semaphore_signal(barrier, inc=1, device_id=device(line(off), p), device_id_type=MESH)
    pl.semaphore_wait(barrier, GROUP + planes - 2)

    def remote(src, dst, send, recv, plane, place):
        return pltpu.make_async_remote_copy(
            src_ref=src, dst_ref=dst, send_sem=send, recv_sem=recv,
            device_id=device(plane, place), device_id_type=MESH,
        )

    def columns(place, c):
        return pl.ds(pl.multiple_of(place * share + c * width, 128), width)

    def piece_copy(c, off):
        return remote(
            hist_ref.at[0, :, columns(peer(off), c)], held[c].at[me],
            piece_send.at[c, off], piece_recv.at[c, p], z, peer(off),
        )

    def own_piece(c):
        return pltpu.make_async_copy(
            hist_ref.at[0, :, columns(p, c)], held[c].at[me], piece_recv.at[c, p]
        )

    def piece_arrival(c, off):
        slot = z * GROUP + peer(off)
        return remote(
            held[c].at[slot], held[c].at[slot],
            piece_send.at[c, off], piece_recv.at[c, peer(off)], z, peer(off),
        )

    def tile_copy(c, off):
        return remote(
            conn_ref.at[:, columns(peer(off), c)], tiles[c].at[p],
            tile_send.at[c, off], tile_recv.at[c, p], z, peer(off),
        )

    def own_tile(c):
        return pltpu.make_async_copy(
            conn_ref.at[:, columns(p, c)], tiles[c].at[p], tile_recv.at[c, p]
        )

    def tile_arrival(c, off):
        return remote(
            tiles[c].at[peer(off)], tiles[c].at[peer(off)],
            tile_send.at[c, off], tile_recv.at[c, peer(off)], z, peer(off),
        )

    def delay_copy(off):
        return remote(
            delay_ref, delay_vmem.at[p], delay_send.at[off], delay_recv.at[p], z, peer(off)
        )

    def delay_arrival(off):
        return remote(
            delay_ref, delay_vmem.at[peer(off)],
            delay_send.at[off], delay_recv.at[peer(off)], z, peer(off),
        )

    def plane_rows(plane):
        return pl.ds(plane * GROUP, GROUP)

    def up_copy(c, k):
        span = held[c].at[plane_rows(z - k)]
        return remote(span, span, up_send.at[c, k], up_recv.at[c, k], z + 1, p)

    def up_arrival(c, k):
        span = held[c].at[plane_rows(z - 1 - k)]
        return remote(span, span, up_send.at[c, k], up_recv.at[c, k], z - 1, p)

    def down_copy(c, k):
        span = held[c].at[plane_rows(z + k)]
        return remote(span, span, down_send.at[c, k], down_recv.at[c, k], z - 1, p)

    def down_arrival(c, k):
        span = held[c].at[plane_rows(z + 1 + k)]
        return remote(span, span, down_send.at[c, k], down_recv.at[c, k], z + 1, p)

    def sends_up(k):
        return (z + 1 < planes) & (z - k >= 0)

    def sends_down(k):
        return (z - 1 >= 0) & (z + k < planes)

    def send_pieces(c):
        own_piece(c).start()
        for off in range(1, GROUP):
            piece_copy(c, off).start()

    def send_tiles(c):
        own_tile(c).start()
        for off in range(1, GROUP):
            tile_copy(c, off).start()

    def forward(c, k):
        @pl.when(sends_up(k))
        def _():
            up_copy(c, k).start()

        @pl.when(sends_down(k))
        def _():
            down_copy(c, k).start()

    def line_stage(c, k):
        @pl.when(z - 1 - k >= 0)
        def _():
            up_arrival(c, k).wait_recv()

        @pl.when(z + 1 + k < planes)
        def _():
            down_arrival(c, k).wait_recv()

        if k + 2 < planes:
            forward(c, k + 1)

    def plane_stage(c):
        own_piece(c).wait()
        for off in range(1, GROUP):
            piece_arrival(c, off).wait_recv()
        forward(c, 0)

    head = head_ref[0]

    def product(c, a):
        total = None
        step = 2 if chunk_blocks % 2 == 0 else 1
        for first in range(0, chunk_blocks, step):
            spans = []
            for b in range(first, first + step):
                base = head + 2 * planes * GROUP - delay_smem[a, 0, p * blocks + c * chunk_blocks + b]
                spans.append(
                    jnp.concatenate(
                        [
                            held[c][
                                lax.rem(base + t, planes * GROUP),
                                :,
                                b * block_cols : (b + 1) * block_cols,
                            ]
                            for t in range(STEPS)
                        ],
                        axis=0,
                    )
                )
            window = jnp.concatenate(spans, axis=1)
            term = lax.dot_general(
                window,
                tiles[c][a, :, first * block_cols : (first + step) * block_cols],
                (((1,), (1,)), ((), ())),
                preferred_element_type=jnp.float32,
            )
            total = term if total is None else total + term
        return total

    def part_copy(off):
        return remote(
            acc.at[peer(off)], parts.at[p], part_send.at[off], part_recv.at[p], z, peer(off)
        )

    def part_arrival(off):
        return remote(
            acc.at[peer(off)], parts.at[peer(off)],
            part_send.at[off], part_recv.at[peer(off)], z, peer(off),
        )

    def compute(c):
        own_tile(c).wait()
        for off in range(1, GROUP):
            tile_arrival(c, off).wait_recv()

        def one(off, carry):
            a = lax.rem(p + 1 + off, GROUP)
            if c == 0:
                acc[a] = product(c, a)
            else:
                acc[a] += product(c, a)
            return carry

        if c < CHUNKS - 1:
            lax.fori_loop(0, GROUP, one, 0)
        else:
            for off in range(GROUP):
                one(off, 0)
                if off < GROUP - 1:
                    part_copy(off + 1).start()

    for off in range(1, GROUP):
        delay_copy(off).start()
    own_delay = pltpu.make_async_copy(delay_ref, delay_vmem.at[p], delay_recv.at[p])
    own_delay.start()
    send_pieces(0)
    send_pieces(1)
    for s in range(CHUNKS + planes - 1):
        if s < CHUNKS:
            plane_stage(s)
            send_tiles(s)
            if s + 2 < CHUNKS:
                send_pieces(s + 2)
        if s == 0:
            own_delay.wait()
            for off in range(1, GROUP):
                delay_arrival(off).wait_recv()
            table = pltpu.make_async_copy(delay_vmem, delay_smem, delay_local)
            table.start()
            table.wait()
        for k in range(planes - 1):
            if 0 <= s - 1 - k < CHUNKS:
                line_stage(s - 1 - k, k)
        if 0 <= s - planes + 1 < CHUNKS:
            compute(s - planes + 1)

    parts[p] = acc[p]
    for off in range(1, GROUP):
        part_arrival(off).wait_recv()

    state = tuple(init_ref[i] for i in range(6))
    outside = outside_ref[...]
    for t in range(STEPS):
        stimulus = parts[0, t * members : (t + 1) * members, :]
        for q in range(1, GROUP):
            stimulus = stimulus + parts[q, t * members : (t + 1) * members, :]
        state = advance(state, stimulus, outside)
        pot[t * members : (t + 1) * members, :] = (state[1] - state[2]).astype(jnp.bfloat16)
    for i in range(6):
        final_ref[i] = state[i]

    count = STEPS * members
    row = lax.broadcasted_iota(jnp.int32, (count, count), 0)
    col = lax.broadcasted_iota(jnp.int32, (count, count), 1)
    order = jnp.where(col == (row % STEPS) * members + row // STEPS, 1.0, 0.0).astype(jnp.bfloat16)
    ordered = jnp.dot(order, pot[...], preferred_element_type=jnp.float32).astype(jnp.bfloat16)
    sensors = lead_ref.shape[1]
    eeg[...] = jnp.dot(ordered, lead_ref[...], preferred_element_type=jnp.float32).reshape(
        planes, GROUP, STEPS, sensors
    )

    def plane_copy(off):
        return remote(
            eeg.at[:, peer(off)], eeg_plane.at[p], plane_send.at[off], plane_recv.at[p], z, peer(off)
        )

    def plane_arrival(off):
        return remote(
            eeg.at[:, peer(off)], eeg_plane.at[peer(off)],
            plane_send.at[off], plane_recv.at[peer(off)], z, peer(off),
        )

    for off in range(1, GROUP):
        plane_copy(off).start()
    eeg_plane[p] = eeg[:, p]
    for off in range(1, GROUP):
        plane_arrival(off).wait_recv()
    over_plane = eeg_plane[0]
    for q in range(1, GROUP):
        over_plane = over_plane + eeg_plane[q]
    eeg_sum[...] = over_plane

    def line_copy(off):
        return remote(
            eeg_sum.at[line(off)], eeg_line.at[z], line_send.at[off], line_recv.at[z], line(off), p
        )

    def line_arrival(off):
        return remote(
            eeg_sum.at[line(off)], eeg_line.at[line(off)],
            line_send.at[off], line_recv.at[line(off)], line(off), p,
        )

    for off in range(1, planes):
        line_copy(off).start()
    eeg_line[z] = eeg_sum[z]
    for off in range(1, planes):
        line_arrival(off).wait_recv()
    over_line = eeg_line[0]
    for q in range(1, planes):
        over_line = over_line + eeg_line[q]
    signal_ref[0] = over_line

    for off in range(1, GROUP):
        delay_copy(off).wait_send()
        part_copy(off).wait_send()
        plane_copy(off).wait_send()
    for off in range(1, planes):
        line_copy(off).wait_send()
    for c in range(CHUNKS):
        for off in range(1, GROUP):
            piece_copy(c, off).wait_send()
            tile_copy(c, off).wait_send()
        for k in range(planes - 1):
            @pl.when(sends_up(k))
            def _(c=c, k=k):
                up_copy(c, k).wait_send()

            @pl.when(sends_down(k))
            def _(c=c, k=k):
                down_copy(c, k).wait_send()


def fused_body(planes, connectome, history, delays, cycle_head, outside_afferent, init_state, lead_field):
    rows, sources = connectome.shape
    members = history.shape[1]
    sensors = lead_field.shape[1]
    slots = planes * GROUP
    share = sources // GROUP
    width = share // CHUNKS
    count = STEPS * members
    dma = pltpu.SemaphoreType.DMA
    f32 = jnp.float32
    vmem = pl.BlockSpec(memory_space=pltpu.VMEM)
    hbm = pl.BlockSpec(memory_space=pl.ANY)
    return pl.pallas_call(
        functools.partial(fused_kernel, planes),
        out_shape=(
            jax.ShapeDtypeStruct((1, STEPS, sensors), f32),
            jax.ShapeDtypeStruct(init_state.shape, f32),
        ),
        in_specs=[hbm, hbm, hbm, pl.BlockSpec(memory_space=pltpu.SMEM), vmem, vmem, vmem],
        out_specs=(vmem, vmem),
        scratch_shapes=[pltpu.VMEM((slots, members, width), jnp.bfloat16) for _ in range(CHUNKS)]
        + [pltpu.VMEM((GROUP, rows, width), jnp.bfloat16) for _ in range(CHUNKS)]
        + [
            pltpu.VMEM((GROUP, 1, delays.shape[1]), jnp.int32),
            pltpu.SMEM((GROUP, 1, delays.shape[1]), jnp.int32),
            pltpu.VMEM((GROUP, count, rows), f32),
            pltpu.VMEM((GROUP, count, rows), f32),
            pltpu.VMEM((count, rows), jnp.bfloat16),
            pltpu.VMEM((planes, GROUP, STEPS, sensors), f32),
            pltpu.VMEM((GROUP, planes, STEPS, sensors), f32),
            pltpu.VMEM((planes, STEPS, sensors), f32),
            pltpu.VMEM((planes, STEPS, sensors), f32),
            dma((CHUNKS, GROUP)),
            dma((CHUNKS, GROUP)),
            dma((CHUNKS, planes)),
            dma((CHUNKS, planes)),
            dma((CHUNKS, planes)),
            dma((CHUNKS, planes)),
            dma((CHUNKS, GROUP)),
            dma((CHUNKS, GROUP)),
            dma((GROUP,)),
            dma((GROUP,)),
            dma,
            dma((GROUP,)),
            dma((GROUP,)),
            dma((GROUP,)),
            dma((GROUP,)),
            dma((planes,)),
            dma((planes,)),
        ],
        compiler_params=pltpu.CompilerParams(
            collective_id=0, has_side_effects=True, vmem_limit_bytes=56 * 1024 * 1024
        ),
        cost_estimate=pl.CostEstimate(
            flops=2 * rows * sources * count, bytes_accessed=4 * rows * sources, transcendentals=0
        ),
    )(
        connectome,
        history,
        delays,
        cycle_head,
        jnp.broadcast_to(outside_afferent[:, None], (members, rows)),
        init_state,
        lead_field,
    )


def solution(mesh):
    in_specs = (
        P("tgt", "src"),
        P("tgt", None, "src"),
        P("tgt", "src"),
        P(),
        P(),
        P(None, None, "tgt"),
        P("tgt", None),
    )
    out_specs = (P("tgt", None, None), P(None, None, ("tgt", "src")))
    devices = mesh.shape["tgt"]
    chosen = body
    if mesh.shape["src"] == 1 and devices % GROUP == 0 and devices > GROUP:
        chosen = functools.partial(fused_body, devices // GROUP)
    return jax.shard_map(chosen, mesh=mesh, in_specs=in_specs, out_specs=out_specs, check_vma=False)
```

```python
import functools

import jax
import jax.numpy as jnp
from jax import lax
from jax.experimental import pallas as pl
from jax.experimental.pallas import tpu as pltpu
from jax.sharding import PartitionSpec as P

STEPS = 16
MESH = pl.DeviceIdType.MESH
GROUP = 8
CHIPS = GROUP // 2
CUTS = (0.28, 0.48, 0.68, 0.88, 1.0)
CHUNKS = len(CUTS)


def chunk_starts(blocks):
    return [0] + [2 * round(cut * blocks / 2) for cut in CUTS[:-1]] + [blocks]


integrator_step_width = 0.1
positive_synaptic_amplitude = 0.0325
negative_synaptic_amplitude = 0.11
interneuron_fraction = 0.5
global_link_scale = 30.0
stellate_contact_count = 135.0
recurrent_loop_contacts = 108.0
interneuron_contact_count = 33.75
peak_spike_rate = 5.0
logistic_slope_factor = 0.56
logistic_midpoint = 6.0


def spike_rate_response(cell_depolarization):
    return peak_spike_rate * jax.nn.sigmoid(
        logistic_slope_factor * (cell_depolarization - logistic_midpoint)
    )


def advance(carry, applied_stimulus, outside_afferent):
    (
        principal_cell_depolarization,
        stellate_mean_depolarization,
        interneuron_mean_depolarization,
        principal_cell_slope,
        excite_rate,
        interneuron_slope,
    ) = carry
    next_principal_cell_slope = principal_cell_slope + integrator_step_width * (
        positive_synaptic_amplitude
        * spike_rate_response(stellate_mean_depolarization - interneuron_mean_depolarization)
        - 2.0 * principal_cell_slope
        - principal_cell_depolarization
    )
    summed_afferent_rate = (
        outside_afferent
        + recurrent_loop_contacts
        * spike_rate_response(stellate_contact_count * principal_cell_depolarization)
        + global_link_scale * applied_stimulus
    )
    new_excite_rate = excite_rate + integrator_step_width * (
        positive_synaptic_amplitude * summed_afferent_rate
        - 2.0 * excite_rate
        - stellate_mean_depolarization
    )
    next_interneuron_slope = interneuron_slope + integrator_step_width * (
        negative_synaptic_amplitude
        * interneuron_contact_count
        * spike_rate_response(interneuron_contact_count * principal_cell_depolarization)
        - 2.0 * interneuron_fraction * interneuron_slope
        - interneuron_fraction * interneuron_fraction * interneuron_mean_depolarization
    )
    return (
        principal_cell_depolarization + integrator_step_width * principal_cell_slope,
        stellate_mean_depolarization + integrator_step_width * excite_rate,
        interneuron_mean_depolarization + integrator_step_width * interneuron_slope,
        next_principal_cell_slope,
        new_excite_rate,
        next_interneuron_slope,
    )


def integrate(init_state, outside_afferent, coupling):

    def one_step(carry, applied_stimulus):
        fresh = advance(carry, applied_stimulus, outside_afferent[:, None])
        return (fresh, fresh[1] - fresh[2])

    begin = tuple((init_state[member] for member in range(6)))
    final, potentials = lax.scan(one_step, begin, coupling)
    return (jnp.stack(final), potentials)


def body(connectome, history, delays, cycle_head, outside_afferent, init_state, lead_field):
    tgt_rows = connectome.shape[0]
    target_blocks = delays.shape[0]
    source_blocks = delays.shape[1]
    block_rows = tgt_rows // target_blocks
    block_cols = connectome.shape[1] // source_blocks
    members = history.shape[1]
    slots_all = history.shape[0] * lax.axis_size("tgt")
    tiles = connectome.reshape(target_blocks, block_rows, source_blocks, block_cols)
    moments = jnp.arange(STEPS, dtype=jnp.int32)
    lag_slot = (cycle_head[0] + moments[None, None, :] - delays[:, :, None]) % slots_all
    whole = lax.all_gather(history, "tgt", axis=0, tiled=True)
    stacked = whole.reshape(slots_all, members, source_blocks, block_cols)
    slot_ids = jnp.arange(slots_all, dtype=jnp.int32)
    wanted = lag_slot[0].T
    picker = (wanted[:, None, :] == slot_ids[None, :, None]).astype(jnp.bfloat16)
    window = jnp.einsum(
        "tkb,kmbs->tmbs", picker, stacked, preferred_element_type=jnp.float32
    ).astype(jnp.bfloat16)
    pieces = jnp.einsum("rbs,tmbs->tmr", tiles[0], window, preferred_element_type=jnp.float32)
    share = tgt_rows // lax.axis_size("src")
    offset_rows = lax.axis_index("src") * share
    summed = lax.psum(pieces, "src")
    final_full, potentials = integrate(init_state, outside_afferent, summed)
    final_state = lax.dynamic_slice_in_dim(final_full, offset_rows, share, 2)
    potential = potentials.astype(jnp.bfloat16)
    signal = lax.psum_scatter(
        jnp.einsum("tmr,rs->mts", potential, lead_field, preferred_element_type=jnp.float32),
        "tgt",
        scatter_dimension=0,
        tiled=True,
    )
    return (signal, final_state)


def fused_kernel(
    planes,
    conn_ref,
    hist_ref,
    delay_ref,
    head_ref,
    outside_ref,
    init_ref,
    lead_ref,
    signal_ref,
    final_ref,
    *scratch,
):
    held = scratch[:CHUNKS]
    tiles = scratch[CHUNKS : 2 * CHUNKS]
    (
        delay_vmem,
        delay_smem,
        other_delay_vmem,
        other_delay_smem,
        other_tiles,
        acc,
        pair,
        parts,
        other_acc,
        other_pair,
        other_parts,
        handed,
        returned,
        coupling,
        pot,
        eeg,
        eeg_plane,
        eeg_sum,
        eeg_line,
        piece_send,
        piece_recv,
        up_send,
        up_recv,
        down_send,
        down_recv,
        tile_send,
        tile_recv,
        delay_send,
        delay_recv,
        delay_local,
        pair_send,
        pair_recv,
        part_send,
        part_recv,
        other_pair_send,
        other_pair_recv,
        other_part_send,
        other_part_recv,
        other_tile_send,
        other_tile_recv,
        other_delay_send,
        other_delay_recv,
        return_send,
        return_recv,
        plane_send,
        plane_recv,
        line_send,
        line_recv,
    ) = scratch[2 * CHUNKS :]
    me = lax.axis_index("tgt")
    z = me // GROUP
    p = me % GROUP
    core = p % 2
    chip = p // 2
    is_end = (z == 0) | (z == planes - 1)
    is_inner = (z > 0) & (z < planes - 1)
    serves = (z == 1) | (z == planes - 2)
    inward = jnp.where(z == 0, 1, planes - 2)
    outward = jnp.where(z == 1, 0, planes - 1)
    rows = conn_ref.shape[0]
    members = hist_ref.shape[1]
    share = conn_ref.shape[1] // GROUP
    blocks = delay_ref.shape[1] // GROUP
    block_cols = share // blocks
    starts = chunk_starts(blocks)

    def peer(off):
        return lax.rem(p + off, GROUP)

    def line(off):
        return lax.rem(z + off, planes)

    def device(plane, place):
        return {"tgt": plane * GROUP + place}

    barrier = pltpu.get_barrier_semaphore()
    for off in range(1, GROUP):
        pl.semaphore_signal(barrier, inc=1, device_id=device(z, peer(off)), device_id_type=MESH)
    for off in range(1, planes):
        pl.semaphore_signal(barrier, inc=1, device_id=device(line(off), p), device_id_type=MESH)
    pl.semaphore_wait(barrier, GROUP + planes - 2)

    def remote(src, dst, send, recv, plane, place):
        return pltpu.make_async_remote_copy(
            src_ref=src, dst_ref=dst, send_sem=send, recv_sem=recv,
            device_id=device(plane, place), device_id_type=MESH,
        )

    def columns(place, c):
        width = (starts[c + 1] - starts[c]) * block_cols
        return pl.ds(pl.multiple_of(place * share + starts[c] * block_cols, 128), width)

    def piece_copy(c, off):
        return remote(
            hist_ref.at[0, :, columns(peer(off), c)], held[c].at[me],
            piece_send.at[c, off], piece_recv.at[c, p], z, peer(off),
        )

    def own_piece(c):
        return pltpu.make_async_copy(
            hist_ref.at[0, :, columns(p, c)], held[c].at[me], piece_recv.at[c, p]
        )

    def piece_arrival(c, off):
        slot = z * GROUP + peer(off)
        return remote(
            held[c].at[slot], held[c].at[slot],
            piece_send.at[c, off], piece_recv.at[c, peer(off)], z, peer(off),
        )

    def tile_copy(c, off):
        return remote(
            conn_ref.at[:, columns(peer(off), c)], tiles[c].at[p],
            tile_send.at[c, off], tile_recv.at[c, p], z, peer(off),
        )

    def own_tile(c):
        return pltpu.make_async_copy(
            conn_ref.at[:, columns(p, c)], tiles[c].at[p], tile_recv.at[c, p]
        )

    def tile_arrival(c, off):
        return remote(
            tiles[c].at[peer(off)], tiles[c].at[peer(off)],
            tile_send.at[c, off], tile_recv.at[c, peer(off)], z, peer(off),
        )

    def delay_copy(off):
        return remote(
            delay_ref, delay_vmem.at[p], delay_send.at[off], delay_recv.at[p], z, peer(off)
        )

    def delay_arrival(off):
        return remote(
            delay_ref, delay_vmem.at[peer(off)],
            delay_send.at[off], delay_recv.at[peer(off)], z, peer(off),
        )

    def plane_rows(plane):
        return pl.ds(plane * GROUP, GROUP)

    def up_copy(c, k):
        span = held[c].at[plane_rows(z - k)]
        return remote(span, span, up_send.at[c, k], up_recv.at[c, k], z + 1, p)

    def up_arrival(c, k):
        span = held[c].at[plane_rows(z - 1 - k)]
        return remote(span, span, up_send.at[c, k], up_recv.at[c, k], z - 1, p)

    def down_copy(c, k):
        span = held[c].at[plane_rows(z + k)]
        return remote(span, span, down_send.at[c, k], down_recv.at[c, k], z - 1, p)

    def down_arrival(c, k):
        span = held[c].at[plane_rows(z + 1 + k)]
        return remote(span, span, down_send.at[c, k], down_recv.at[c, k], z + 1, p)

    def edge(c):
        return 1 if c == 0 else 0

    def sends_up(c, k):
        return (z + 1 < planes - edge(c)) & (z - k >= 0)

    def sends_down(c, k):
        return (z - 1 >= edge(c)) & (z + k < planes)

    def send_pieces(c):
        own_piece(c).start()
        for off in range(1, GROUP):
            piece_copy(c, off).start()

    def send_tiles(c):
        own_tile(c).start()
        for off in range(1, GROUP):
            tile_copy(c, off).start()

    def forward(c, k):
        @pl.when(sends_up(c, k))
        def _():
            up_copy(c, k).start()

        @pl.when(sends_down(c, k))
        def _():
            down_copy(c, k).start()

    def line_stage(c, k):
        @pl.when((z - 1 - k >= 0) & (z < planes - edge(c)))
        def _():
            up_arrival(c, k).wait_recv()

        @pl.when((z + 1 + k < planes) & (z >= edge(c)))
        def _():
            down_arrival(c, k).wait_recv()

        if k + 2 < planes:
            forward(c, k + 1)

    def plane_stage(c):
        own_piece(c).wait()
        for off in range(1, GROUP):
            piece_arrival(c, off).wait_recv()
        forward(c, 0)

    head = head_ref[0]

    def product(c, a, tile, table):
        total = None
        count = starts[c + 1] - starts[c]
        for first in range(0, count, 2):
            last = min(first + 2, count)
            spans = []
            for b in range(first, last):
                base = head + 2 * planes * GROUP - table[a, 0, p * blocks + starts[c] + b]
                spans.append(
                    jnp.concatenate(
                        [
                            held[c][
                                lax.rem(base + t, planes * GROUP),
                                :,
                                b * block_cols : (b + 1) * block_cols,
                            ]
                            for t in range(STEPS)
                        ],
                        axis=0,
                    )
                )
            window = jnp.concatenate(spans, axis=1)
            term = lax.dot_general(
                window,
                tile[a, :, first * block_cols : last * block_cols],
                (((1,), (1,)), ((), ())),
                preferred_element_type=jnp.float32,
            )
            total = term if total is None else total + term
        return total

    class Sum:
        def __init__(self, own, pair, parts, pair_send, pair_recv, part_send, part_recv):
            self.own, self.pair, self.parts = own, pair, parts
            self.pair_send, self.pair_recv = pair_send, pair_recv
            self.part_send, self.part_recv = part_send, part_recv

        def pair_copy(self, j):
            return remote(
                self.own.at[2 * j + 1 - core], self.pair.at[j],
                self.pair_send.at[j], self.pair_recv.at[j], z, 2 * chip + 1 - core,
            )

        def part_copy(self, off):
            j = lax.rem(chip + off, CHIPS)
            return remote(
                self.own.at[2 * j + core], self.parts.at[chip],
                self.part_send.at[off], self.part_recv.at[chip], z, 2 * j + core,
            )

        def part_arrival(self, off):
            j = lax.rem(chip + off, CHIPS)
            return remote(
                self.own.at[2 * j + core], self.parts.at[j],
                self.part_send.at[off], self.part_recv.at[j], z, 2 * j + core,
            )

        def pass_on(self, off):
            j = lax.rem(chip + off, CHIPS)
            self.pair_copy(j).wait_recv()
            self.own[2 * j + core] += self.pair[j]
            if off > 0:
                self.part_copy(off).start()

        def send(self, fill):
            order = list(range(1, CHIPS)) + [0]
            for at, off in enumerate(order):
                j = lax.rem(chip + off, CHIPS)
                fill(2 * j + 1 - core)
                self.pair_copy(j).start()
                fill(2 * j + core)
                if at > 0:
                    self.pass_on(order[at - 1])
            self.pass_on(order[-1])

        def total(self):
            value = self.own[2 * chip + core]
            for off in range(1, CHIPS):
                self.part_arrival(off).wait_recv()
                value = value + self.parts[lax.rem(chip + off, CHIPS)]
            return value

        def finish(self):
            for j in range(CHIPS):
                self.pair_copy(j).wait_send()
            for off in range(1, CHIPS):
                self.part_copy(off).wait_send()

    main = Sum(acc, pair, parts, pair_send, pair_recv, part_send, part_recv)
    other = Sum(
        other_acc, other_pair, other_parts,
        other_pair_send, other_pair_recv, other_part_send, other_part_recv,
    )

    def tiles_arrive(c):
        own_tile(c).wait()
        for off in range(1, GROUP):
            tile_arrival(c, off).wait_recv()

    def compute(c):
        tiles_arrive(c)

        def one(a):
            acc[a] += product(c, a, tiles[c], delay_smem)

        if c < CHUNKS - 1:
            lax.fori_loop(0, GROUP, lambda a, carry: (one(a), carry)[1], 0)
        else:
            main.send(one)

    def other_tile_copy(a, plane):
        return remote(
            tiles[0].at[a], other_tiles.at[a], other_tile_send.at[a], other_tile_recv.at[a], plane, p
        )

    def other_delay_copy(plane):
        return remote(
            delay_vmem, other_delay_vmem, other_delay_send, other_delay_recv, plane, p
        )

    def hand_over():
        other_delay_copy(inward).start()
        own_tile(0).wait()
        other_tile_copy(p, inward).start()
        for off in range(1, GROUP):
            tile_arrival(0, off).wait_recv()
            other_tile_copy(peer(off), inward).start()

    def compute_other():
        other_delay_copy(outward).wait_recv()
        table = pltpu.make_async_copy(other_delay_vmem, other_delay_smem, delay_local)
        table.start()
        table.wait()
        for a in range(GROUP):
            other_tile_copy(a, outward).wait_recv()

        def one(a):
            other_acc[a] = product(0, a, other_tiles, other_delay_smem)

        other.send(one)

    def return_copy(plane):
        return remote(handed, returned, return_send, return_recv, plane, p)

    def return_other():
        handed[...] = other.total()
        return_copy(outward).start()

    for off in range(1, GROUP):
        delay_copy(off).start()
    own_delay = pltpu.make_async_copy(delay_ref, delay_vmem.at[p], delay_recv.at[p])
    own_delay.start()
    send_pieces(0)

    @pl.when(is_end)
    def _():
        send_tiles(0)

    send_pieces(1)

    @pl.when(is_inner)
    def _():
        send_tiles(0)

    acc[...] = jnp.zeros_like(acc)
    for s in range(CHUNKS + planes - 1):
        if s < CHUNKS:
            plane_stage(s)
            if s + 2 < CHUNKS:
                send_pieces(s + 2)
            if s + 1 < CHUNKS:
                send_tiles(s + 1)
        if s == 0:
            own_delay.wait()
            for off in range(1, GROUP):
                delay_arrival(off).wait_recv()
            table = pltpu.make_async_copy(delay_vmem, delay_smem, delay_local)
            table.start()
            table.wait()
            pl.when(is_end)(hand_over)
        for k in range(planes - 1):
            if 0 <= s - 1 - k < CHUNKS:
                line_stage(s - 1 - k, k)
        if s == planes + 2:
            pl.when(serves)(return_other)
        c = s - planes + 1
        if c == 0:
            pl.when(is_inner)(functools.partial(compute, 0))
        elif 0 < c < CHUNKS:
            compute(c)
        if s == planes:
            pl.when(serves)(compute_other)

    coupling[...] = main.total()

    @pl.when(is_end)
    def _():
        return_copy(inward).wait_recv()
        coupling[...] += returned[...]

    state = tuple(init_ref[i] for i in range(6))
    member = lax.broadcasted_iota(jnp.int32, (members, rows), 0)
    outside = jnp.zeros((members, rows), jnp.float32)
    for m in range(members):
        outside = jnp.where(member == m, outside_ref[m], outside)
    for t in range(STEPS):
        stimulus = coupling[t * members : (t + 1) * members, :]
        state = advance(state, stimulus, outside)
        pot[t * members : (t + 1) * members, :] = (state[1] - state[2]).astype(jnp.bfloat16)
    for i in range(6):
        final_ref[i] = state[i]

    count = STEPS * members
    row = lax.broadcasted_iota(jnp.int32, (count, count), 0)
    col = lax.broadcasted_iota(jnp.int32, (count, count), 1)
    order = jnp.where(col == (row % STEPS) * members + row // STEPS, 1.0, 0.0).astype(jnp.bfloat16)
    ordered = jnp.dot(order, pot[...], preferred_element_type=jnp.float32).astype(jnp.bfloat16)
    sensors = lead_ref.shape[1]
    eeg[...] = jnp.dot(ordered, lead_ref[...], preferred_element_type=jnp.float32).reshape(
        planes, GROUP, STEPS, sensors
    )

    def plane_copy(off):
        return remote(
            eeg.at[:, peer(off)], eeg_plane.at[p], plane_send.at[off], plane_recv.at[p], z, peer(off)
        )

    def plane_arrival(off):
        return remote(
            eeg.at[:, peer(off)], eeg_plane.at[peer(off)],
            plane_send.at[off], plane_recv.at[peer(off)], z, peer(off),
        )

    for off in range(1, GROUP):
        plane_copy(off).start()
    eeg_plane[p] = eeg[:, p]
    for off in range(1, GROUP):
        plane_arrival(off).wait_recv()
    over_plane = eeg_plane[0]
    for q in range(1, GROUP):
        over_plane = over_plane + eeg_plane[q]
    eeg_sum[...] = over_plane

    def line_copy(off):
        return remote(
            eeg_sum.at[line(off)], eeg_line.at[z], line_send.at[off], line_recv.at[z], line(off), p
        )

    def line_arrival(off):
        return remote(
            eeg_sum.at[line(off)], eeg_line.at[line(off)],
            line_send.at[off], line_recv.at[line(off)], line(off), p,
        )

    for off in range(1, planes):
        line_copy(off).start()
    eeg_line[z] = eeg_sum[z]
    for off in range(1, planes):
        line_arrival(off).wait_recv()
    over_line = eeg_line[0]
    for q in range(1, planes):
        over_line = over_line + eeg_line[q]
    signal_ref[0] = over_line

    for off in range(1, GROUP):
        delay_copy(off).wait_send()
        plane_copy(off).wait_send()
    main.finish()

    @pl.when(is_end)
    def _():
        other_delay_copy(inward).wait_send()
        for a in range(GROUP):
            other_tile_copy(a, inward).wait_send()

    @pl.when(serves)
    def _():
        other.finish()
        return_copy(outward).wait_send()

    for off in range(1, planes):
        line_copy(off).wait_send()
    for c in range(CHUNKS):
        for off in range(1, GROUP):
            piece_copy(c, off).wait_send()
            tile_copy(c, off).wait_send()
        for k in range(planes - 1):
            @pl.when(sends_up(c, k))
            def _(c=c, k=k):
                up_copy(c, k).wait_send()

            @pl.when(sends_down(c, k))
            def _(c=c, k=k):
                down_copy(c, k).wait_send()


def fused_body(planes, connectome, history, delays, cycle_head, outside_afferent, init_state, lead_field):
    rows, sources = connectome.shape
    members = history.shape[1]
    sensors = lead_field.shape[1]
    slots = planes * GROUP
    share = sources // GROUP
    blocks = delays.shape[1] // GROUP
    starts = chunk_starts(blocks)
    widths = [(stop - start) * (share // blocks) for start, stop in zip(starts, starts[1:])]
    count = STEPS * members
    dma = pltpu.SemaphoreType.DMA
    f32 = jnp.float32
    vmem = pl.BlockSpec(memory_space=pltpu.VMEM)
    smem = pl.BlockSpec(memory_space=pltpu.SMEM)
    hbm = pl.BlockSpec(memory_space=pl.ANY)
    return pl.pallas_call(
        functools.partial(fused_kernel, planes),
        out_shape=(
            jax.ShapeDtypeStruct((1, STEPS, sensors), f32),
            jax.ShapeDtypeStruct(init_state.shape, f32),
        ),
        in_specs=[hbm, hbm, hbm, smem, smem, vmem, vmem],
        out_specs=(vmem, vmem),
        scratch_shapes=[pltpu.VMEM((slots, members, width), jnp.bfloat16) for width in widths]
        + [pltpu.VMEM((GROUP, rows, width), jnp.bfloat16) for width in widths]
        + [
            pltpu.VMEM((GROUP, 1, delays.shape[1]), jnp.int32),
            pltpu.SMEM((GROUP, 1, delays.shape[1]), jnp.int32),
            pltpu.VMEM((GROUP, 1, delays.shape[1]), jnp.int32),
            pltpu.SMEM((GROUP, 1, delays.shape[1]), jnp.int32),
            pltpu.VMEM((GROUP, rows, widths[0]), jnp.bfloat16),
            pltpu.VMEM((GROUP, count, rows), f32),
            pltpu.VMEM((CHIPS, count, rows), f32),
            pltpu.VMEM((CHIPS, count, rows), f32),
            pltpu.VMEM((GROUP, count, rows), f32),
            pltpu.VMEM((CHIPS, count, rows), f32),
            pltpu.VMEM((CHIPS, count, rows), f32),
            pltpu.VMEM((count, rows), f32),
            pltpu.VMEM((count, rows), f32),
            pltpu.VMEM((count, rows), f32),
            pltpu.VMEM((count, rows), jnp.bfloat16),
            pltpu.VMEM((planes, GROUP, STEPS, sensors), f32),
            pltpu.VMEM((GROUP, planes, STEPS, sensors), f32),
            pltpu.VMEM((planes, STEPS, sensors), f32),
            pltpu.VMEM((planes, STEPS, sensors), f32),
            dma((CHUNKS, GROUP)),
            dma((CHUNKS, GROUP)),
            dma((CHUNKS, planes)),
            dma((CHUNKS, planes)),
            dma((CHUNKS, planes)),
            dma((CHUNKS, planes)),
            dma((CHUNKS, GROUP)),
            dma((CHUNKS, GROUP)),
            dma((GROUP,)),
            dma((GROUP,)),
            dma,
            dma((CHIPS,)),
            dma((CHIPS,)),
            dma((CHIPS,)),
            dma((CHIPS,)),
            dma((CHIPS,)),
            dma((CHIPS,)),
            dma((CHIPS,)),
            dma((CHIPS,)),
            dma((GROUP,)),
            dma((GROUP,)),
            dma,
            dma,
            dma,
            dma,
            dma((GROUP,)),
            dma((GROUP,)),
            dma((planes,)),
            dma((planes,)),
        ],
        compiler_params=pltpu.CompilerParams(
            collective_id=0, has_side_effects=True, vmem_limit_bytes=56 * 1024 * 1024
        ),
        cost_estimate=pl.CostEstimate(
            flops=2 * rows * sources * count, bytes_accessed=4 * rows * sources, transcendentals=0
        ),
    )(
        connectome,
        history,
        delays,
        cycle_head,
        outside_afferent,
        init_state,
        lead_field,
    )


def solution(mesh):
    in_specs = (
        P("tgt", "src"),
        P("tgt", None, "src"),
        P("tgt", "src"),
        P(),
        P(),
        P(None, None, "tgt"),
        P("tgt", None),
    )
    out_specs = (P("tgt", None, None), P(None, None, ("tgt", "src")))
    devices = mesh.shape["tgt"]
    chosen = body
    if mesh.shape["src"] == 1 and devices % GROUP == 0 and devices >= 4 * GROUP:
        chosen = functools.partial(fused_body, devices // GROUP)
    return jax.shard_map(chosen, mesh=mesh, in_specs=in_specs, out_specs=out_specs, check_vma=False)
```

```python
import functools

import jax
import jax.numpy as jnp
from jax import lax
from jax.experimental import pallas as pl
from jax.experimental.pallas import tpu as pltpu
from jax.sharding import PartitionSpec as P

STEPS = 16
MESH = pl.DeviceIdType.MESH
GROUP = 8
CHIPS = GROUP // 2
CUTS = (0.2, 0.44, 0.68, 0.88, 1.0)
CHUNKS = len(CUTS)


def chunk_starts(blocks):
    return [0] + [2 * round(cut * blocks / 2) for cut in CUTS[:-1]] + [blocks]


integrator_step_width = 0.1
positive_synaptic_amplitude = 0.0325
negative_synaptic_amplitude = 0.11
interneuron_fraction = 0.5
global_link_scale = 30.0
stellate_contact_count = 135.0
recurrent_loop_contacts = 108.0
interneuron_contact_count = 33.75
peak_spike_rate = 5.0
logistic_slope_factor = 0.56
logistic_midpoint = 6.0


def spike_rate_response(cell_depolarization):
    return peak_spike_rate * jax.nn.sigmoid(
        logistic_slope_factor * (cell_depolarization - logistic_midpoint)
    )


def advance(carry, applied_stimulus, outside_afferent):
    (
        principal_cell_depolarization,
        stellate_mean_depolarization,
        interneuron_mean_depolarization,
        principal_cell_slope,
        excite_rate,
        interneuron_slope,
    ) = carry
    next_principal_cell_slope = principal_cell_slope + integrator_step_width * (
        positive_synaptic_amplitude
        * spike_rate_response(stellate_mean_depolarization - interneuron_mean_depolarization)
        - 2.0 * principal_cell_slope
        - principal_cell_depolarization
    )
    summed_afferent_rate = (
        outside_afferent
        + recurrent_loop_contacts
        * spike_rate_response(stellate_contact_count * principal_cell_depolarization)
        + global_link_scale * applied_stimulus
    )
    new_excite_rate = excite_rate + integrator_step_width * (
        positive_synaptic_amplitude * summed_afferent_rate
        - 2.0 * excite_rate
        - stellate_mean_depolarization
    )
    next_interneuron_slope = interneuron_slope + integrator_step_width * (
        negative_synaptic_amplitude
        * interneuron_contact_count
        * spike_rate_response(interneuron_contact_count * principal_cell_depolarization)
        - 2.0 * interneuron_fraction * interneuron_slope
        - interneuron_fraction * interneuron_fraction * interneuron_mean_depolarization
    )
    return (
        principal_cell_depolarization + integrator_step_width * principal_cell_slope,
        stellate_mean_depolarization + integrator_step_width * excite_rate,
        interneuron_mean_depolarization + integrator_step_width * interneuron_slope,
        next_principal_cell_slope,
        new_excite_rate,
        next_interneuron_slope,
    )


def integrate(init_state, outside_afferent, coupling):

    def one_step(carry, applied_stimulus):
        fresh = advance(carry, applied_stimulus, outside_afferent[:, None])
        return (fresh, fresh[1] - fresh[2])

    begin = tuple((init_state[member] for member in range(6)))
    final, potentials = lax.scan(one_step, begin, coupling)
    return (jnp.stack(final), potentials)


def body(connectome, history, delays, cycle_head, outside_afferent, init_state, lead_field):
    tgt_rows = connectome.shape[0]
    target_blocks = delays.shape[0]
    source_blocks = delays.shape[1]
    block_rows = tgt_rows // target_blocks
    block_cols = connectome.shape[1] // source_blocks
    members = history.shape[1]
    slots_all = history.shape[0] * lax.axis_size("tgt")
    tiles = connectome.reshape(target_blocks, block_rows, source_blocks, block_cols)
    moments = jnp.arange(STEPS, dtype=jnp.int32)
    lag_slot = (cycle_head[0] + moments[None, None, :] - delays[:, :, None]) % slots_all
    whole = lax.all_gather(history, "tgt", axis=0, tiled=True)
    stacked = whole.reshape(slots_all, members, source_blocks, block_cols)
    slot_ids = jnp.arange(slots_all, dtype=jnp.int32)
    wanted = lag_slot[0].T
    picker = (wanted[:, None, :] == slot_ids[None, :, None]).astype(jnp.bfloat16)
    window = jnp.einsum(
        "tkb,kmbs->tmbs", picker, stacked, preferred_element_type=jnp.float32
    ).astype(jnp.bfloat16)
    pieces = jnp.einsum("rbs,tmbs->tmr", tiles[0], window, preferred_element_type=jnp.float32)
    share = tgt_rows // lax.axis_size("src")
    offset_rows = lax.axis_index("src") * share
    summed = lax.psum(pieces, "src")
    final_full, potentials = integrate(init_state, outside_afferent, summed)
    final_state = lax.dynamic_slice_in_dim(final_full, offset_rows, share, 2)
    potential = potentials.astype(jnp.bfloat16)
    signal = lax.psum_scatter(
        jnp.einsum("tmr,rs->mts", potential, lead_field, preferred_element_type=jnp.float32),
        "tgt",
        scatter_dimension=0,
        tiled=True,
    )
    return (signal, final_state)


def fused_kernel(
    planes,
    conn_ref,
    hist_ref,
    delay_ref,
    head_ref,
    outside_ref,
    init_ref,
    lead_ref,
    signal_ref,
    final_ref,
    *scratch,
):
    held = scratch[:CHUNKS]
    tiles = scratch[CHUNKS : 2 * CHUNKS]
    (
        delay_vmem,
        delay_smem,
        acc,
        pair,
        parts,
        coupling,
        pot,
        eeg,
        eeg_plane,
        eeg_sum,
        eeg_line,
        piece_send,
        piece_recv,
        up_send,
        up_recv,
        down_send,
        down_recv,
        tile_send,
        tile_recv,
        delay_send,
        delay_recv,
        delay_local,
        pair_send,
        pair_recv,
        part_send,
        part_recv,
        plane_send,
        plane_recv,
        line_send,
        line_recv,
    ) = scratch[2 * CHUNKS :]
    me = lax.axis_index("tgt")
    z = me // GROUP
    p = me % GROUP
    core = p % 2
    chip = p // 2
    is_end = (z == 0) | (z == planes - 1)
    is_inner = (z > 0) & (z < planes - 1)
    rows = conn_ref.shape[0]
    members = hist_ref.shape[1]
    share = conn_ref.shape[1] // GROUP
    blocks = delay_ref.shape[1] // GROUP
    block_cols = share // blocks
    starts = chunk_starts(blocks)

    def peer(off):
        return lax.rem(p + off, GROUP)

    def line(off):
        return lax.rem(z + off, planes)

    def device(plane, place):
        return {"tgt": plane * GROUP + place}

    barrier = pltpu.get_barrier_semaphore()
    for off in range(1, GROUP):
        pl.semaphore_signal(barrier, inc=1, device_id=device(z, peer(off)), device_id_type=MESH)
    for off in range(1, planes):
        pl.semaphore_signal(barrier, inc=1, device_id=device(line(off), p), device_id_type=MESH)
    pl.semaphore_wait(barrier, GROUP + planes - 2)

    def remote(src, dst, send, recv, plane, place):
        return pltpu.make_async_remote_copy(
            src_ref=src, dst_ref=dst, send_sem=send, recv_sem=recv,
            device_id=device(plane, place), device_id_type=MESH,
        )

    def columns(place, c):
        width = (starts[c + 1] - starts[c]) * block_cols
        return pl.ds(pl.multiple_of(place * share + starts[c] * block_cols, 128), width)

    def piece_copy(c, off):
        return remote(
            hist_ref.at[0, :, columns(peer(off), c)], held[c].at[me],
            piece_send.at[c, off], piece_recv.at[c, p], z, peer(off),
        )

    def own_piece(c):
        return pltpu.make_async_copy(
            hist_ref.at[0, :, columns(p, c)], held[c].at[me], piece_recv.at[c, p]
        )

    def piece_arrival(c, off):
        slot = z * GROUP + peer(off)
        return remote(
            held[c].at[slot], held[c].at[slot],
            piece_send.at[c, off], piece_recv.at[c, peer(off)], z, peer(off),
        )

    def tile_copy(c, off):
        return remote(
            conn_ref.at[:, columns(peer(off), c)], tiles[c].at[p],
            tile_send.at[c, off], tile_recv.at[c, p], z, peer(off),
        )

    def own_tile(c):
        return pltpu.make_async_copy(
            conn_ref.at[:, columns(p, c)], tiles[c].at[p], tile_recv.at[c, p]
        )

    def tile_arrival(c, off):
        return remote(
            tiles[c].at[peer(off)], tiles[c].at[peer(off)],
            tile_send.at[c, off], tile_recv.at[c, peer(off)], z, peer(off),
        )

    def delay_copy(off):
        return remote(
            delay_ref, delay_vmem.at[p], delay_send.at[off], delay_recv.at[p], z, peer(off)
        )

    def delay_arrival(off):
        return remote(
            delay_ref, delay_vmem.at[peer(off)],
            delay_send.at[off], delay_recv.at[peer(off)], z, peer(off),
        )

    def plane_rows(plane):
        return pl.ds(plane * GROUP, GROUP)

    def up_copy(c, k):
        span = held[c].at[plane_rows(z - k)]
        return remote(span, span, up_send.at[c, k], up_recv.at[c, k], z + 1, p)

    def up_arrival(c, k):
        span = held[c].at[plane_rows(z - 1 - k)]
        return remote(span, span, up_send.at[c, k], up_recv.at[c, k], z - 1, p)

    def down_copy(c, k):
        span = held[c].at[plane_rows(z + k)]
        return remote(span, span, down_send.at[c, k], down_recv.at[c, k], z - 1, p)

    def down_arrival(c, k):
        span = held[c].at[plane_rows(z + 1 + k)]
        return remote(span, span, down_send.at[c, k], down_recv.at[c, k], z + 1, p)

    def sends_up(k):
        return (z + 1 < planes) & (z - k >= 0)

    def sends_down(k):
        return (z - 1 >= 0) & (z + k < planes)

    def send_pieces(c):
        own_piece(c).start()
        for off in range(1, GROUP):
            piece_copy(c, off).start()

    def send_tiles(c):
        own_tile(c).start()
        for off in range(1, GROUP):
            tile_copy(c, off).start()

    def forward(c, k):
        @pl.when(sends_up(k))
        def _():
            up_copy(c, k).start()

        @pl.when(sends_down(k))
        def _():
            down_copy(c, k).start()

    def line_arrives(c, k, here):
        @pl.when((z - 1 - k >= 0) & here)
        def _():
            up_arrival(c, k).wait_recv()

        @pl.when((z + 1 + k < planes) & here)
        def _():
            down_arrival(c, k).wait_recv()

    def line_stage(c, k):
        line_arrives(c, k, is_inner)
        if k + 2 < planes:
            forward(c, k + 1)

    def plane_stage(c):
        own_piece(c).wait()
        for off in range(1, GROUP):
            piece_arrival(c, off).wait_recv()
        forward(c, 0)

    head = head_ref[0]

    slots = planes * GROUP

    def slot_of(at):
        return at & (slots - 1) if slots & (slots - 1) == 0 else lax.rem(at, slots)

    def product(c, a, tile, table):
        total = None
        count = starts[c + 1] - starts[c]
        for first in range(0, count, 2):
            last = min(first + 2, count)
            spans = []
            for b in range(first, last):
                base = head + 2 * slots - table[a, 0, p * blocks + starts[c] + b]
                spans.append(
                    jnp.concatenate(
                        [
                            held[c][
                                slot_of(base + t),
                                :,
                                b * block_cols : (b + 1) * block_cols,
                            ]
                            for t in range(STEPS)
                        ],
                        axis=0,
                    )
                )
            window = jnp.concatenate(spans, axis=1)
            term = lax.dot_general(
                window,
                tile[a, :, first * block_cols : last * block_cols],
                (((1,), (1,)), ((), ())),
                preferred_element_type=jnp.float32,
            )
            total = term if total is None else total + term
        return total

    class Sum:
        def __init__(self, own, pair, parts, pair_send, pair_recv, part_send, part_recv):
            self.own, self.pair, self.parts = own, pair, parts
            self.pair_send, self.pair_recv = pair_send, pair_recv
            self.part_send, self.part_recv = part_send, part_recv

        def pair_copy(self, j):
            return remote(
                self.own.at[2 * j + 1 - core], self.pair.at[j],
                self.pair_send.at[j], self.pair_recv.at[j], z, 2 * chip + 1 - core,
            )

        def part_copy(self, off):
            j = lax.rem(chip + off, CHIPS)
            return remote(
                self.own.at[2 * j + core], self.parts.at[chip],
                self.part_send.at[off], self.part_recv.at[chip], z, 2 * j + core,
            )

        def part_arrival(self, off):
            j = lax.rem(chip + off, CHIPS)
            return remote(
                self.own.at[2 * j + core], self.parts.at[j],
                self.part_send.at[off], self.part_recv.at[j], z, 2 * j + core,
            )

        def pass_on(self, off):
            j = lax.rem(chip + off, CHIPS)
            self.pair_copy(j).wait_recv()
            self.own[2 * j + core] += self.pair[j]
            if off > 0:
                self.part_copy(off).start()

        def send(self, fill):
            order = list(range(1, CHIPS)) + [0]
            for at, off in enumerate(order):
                j = lax.rem(chip + off, CHIPS)
                fill(2 * j + 1 - core)
                self.pair_copy(j).start()
                fill(2 * j + core)
                if at > 0:
                    self.pass_on(order[at - 1])
            self.pass_on(order[-1])

        def total(self):
            value = self.own[2 * chip + core]
            for off in range(1, CHIPS):
                self.part_arrival(off).wait_recv()
                value = value + self.parts[lax.rem(chip + off, CHIPS)]
            return value

        def finish(self):
            for j in range(CHIPS):
                self.pair_copy(j).wait_send()
            for off in range(1, CHIPS):
                self.part_copy(off).wait_send()

    main = Sum(acc, pair, parts, pair_send, pair_recv, part_send, part_recv)
    def tiles_arrive(c):
        own_tile(c).wait()
        for off in range(1, GROUP):
            tile_arrival(c, off).wait_recv()

    def compute(c):
        tiles_arrive(c)
        for k in range(planes - 1):
            line_arrives(c, k, is_end)

        def one(a):
            acc[a] += product(c, a, tiles[c], delay_smem)

        if c < CHUNKS - 1:
            lax.fori_loop(0, GROUP, lambda a, carry: (one(a), carry)[1], 0)
        else:
            main.send(one)

    for off in range(1, GROUP):
        delay_copy(off).start()
    own_delay = pltpu.make_async_copy(delay_ref, delay_vmem.at[p], delay_recv.at[p])
    own_delay.start()
    send_pieces(0)
    send_pieces(1)
    send_tiles(0)
    acc[...] = jnp.zeros_like(acc)
    for s in range(CHUNKS + planes - 1):
        if s < CHUNKS:
            plane_stage(s)
            if s + 2 < CHUNKS:
                send_pieces(s + 2)
            if s + 1 < CHUNKS:
                send_tiles(s + 1)
        if s == 0:
            own_delay.wait()
            for off in range(1, GROUP):
                delay_arrival(off).wait_recv()
            table = pltpu.make_async_copy(delay_vmem, delay_smem, delay_local)
            table.start()
            table.wait()
        for k in range(planes - 1):
            if 0 <= s - 1 - k < CHUNKS:
                line_stage(s - 1 - k, k)
        if 0 <= s - planes + 1 < CHUNKS:
            compute(s - planes + 1)

    coupling[...] = main.total()

    state = tuple(init_ref[i] for i in range(6))
    member = lax.broadcasted_iota(jnp.int32, (members, rows), 0)
    outside = jnp.zeros((members, rows), jnp.float32)
    for m in range(members):
        outside = jnp.where(member == m, outside_ref[m], outside)
    for t in range(STEPS):
        stimulus = coupling[t * members : (t + 1) * members, :]
        state = advance(state, stimulus, outside)
        pot[t * members : (t + 1) * members, :] = (state[1] - state[2]).astype(jnp.bfloat16)
    for i in range(6):
        final_ref[i] = state[i]

    count = STEPS * members
    row = lax.broadcasted_iota(jnp.int32, (count, count), 0)
    col = lax.broadcasted_iota(jnp.int32, (count, count), 1)
    order = jnp.where(col == (row % STEPS) * members + row // STEPS, 1.0, 0.0).astype(jnp.bfloat16)
    ordered = jnp.dot(order, pot[...], preferred_element_type=jnp.float32).astype(jnp.bfloat16)
    sensors = lead_ref.shape[1]
    eeg[...] = jnp.dot(ordered, lead_ref[...], preferred_element_type=jnp.float32).reshape(
        planes, GROUP, STEPS, sensors
    )

    def plane_copy(off):
        return remote(
            eeg.at[:, peer(off)], eeg_plane.at[p], plane_send.at[off], plane_recv.at[p], z, peer(off)
        )

    def plane_arrival(off):
        return remote(
            eeg.at[:, peer(off)], eeg_plane.at[peer(off)],
            plane_send.at[off], plane_recv.at[peer(off)], z, peer(off),
        )

    for off in range(1, GROUP):
        plane_copy(off).start()
    eeg_plane[p] = eeg[:, p]
    for off in range(1, GROUP):
        plane_arrival(off).wait_recv()
    over_plane = eeg_plane[0]
    for q in range(1, GROUP):
        over_plane = over_plane + eeg_plane[q]
    eeg_sum[...] = over_plane

    def line_copy(off):
        return remote(
            eeg_sum.at[line(off)], eeg_line.at[z], line_send.at[off], line_recv.at[z], line(off), p
        )

    def line_arrival(off):
        return remote(
            eeg_sum.at[line(off)], eeg_line.at[line(off)],
            line_send.at[off], line_recv.at[line(off)], line(off), p,
        )

    for off in range(1, planes):
        line_copy(off).start()
    eeg_line[z] = eeg_sum[z]
    for off in range(1, planes):
        line_arrival(off).wait_recv()
    over_line = eeg_line[0]
    for q in range(1, planes):
        over_line = over_line + eeg_line[q]
    signal_ref[0] = over_line

    for off in range(1, GROUP):
        delay_copy(off).wait_send()
        plane_copy(off).wait_send()
    main.finish()

    for off in range(1, planes):
        line_copy(off).wait_send()
    for c in range(CHUNKS):
        for off in range(1, GROUP):
            piece_copy(c, off).wait_send()
            tile_copy(c, off).wait_send()
        for k in range(planes - 1):
            @pl.when(sends_up(k))
            def _(c=c, k=k):
                up_copy(c, k).wait_send()

            @pl.when(sends_down(k))
            def _(c=c, k=k):
                down_copy(c, k).wait_send()


def fused_body(planes, connectome, history, delays, cycle_head, outside_afferent, init_state, lead_field):
    rows, sources = connectome.shape
    members = history.shape[1]
    sensors = lead_field.shape[1]
    slots = planes * GROUP
    share = sources // GROUP
    blocks = delays.shape[1] // GROUP
    starts = chunk_starts(blocks)
    widths = [(stop - start) * (share // blocks) for start, stop in zip(starts, starts[1:])]
    count = STEPS * members
    dma = pltpu.SemaphoreType.DMA
    f32 = jnp.float32
    vmem = pl.BlockSpec(memory_space=pltpu.VMEM)
    smem = pl.BlockSpec(memory_space=pltpu.SMEM)
    hbm = pl.BlockSpec(memory_space=pl.ANY)
    return pl.pallas_call(
        functools.partial(fused_kernel, planes),
        out_shape=(
            jax.ShapeDtypeStruct((1, STEPS, sensors), f32),
            jax.ShapeDtypeStruct(init_state.shape, f32),
        ),
        in_specs=[hbm, hbm, hbm, smem, smem, vmem, vmem],
        out_specs=(vmem, vmem),
        scratch_shapes=[pltpu.VMEM((slots, members, width), jnp.bfloat16) for width in widths]
        + [pltpu.VMEM((GROUP, rows, width), jnp.bfloat16) for width in widths]
        + [
            pltpu.VMEM((GROUP, 1, delays.shape[1]), jnp.int32),
            pltpu.SMEM((GROUP, 1, delays.shape[1]), jnp.int32),
            pltpu.VMEM((GROUP, count, rows), f32),
            pltpu.VMEM((CHIPS, count, rows), f32),
            pltpu.VMEM((CHIPS, count, rows), f32),
            pltpu.VMEM((count, rows), f32),
            pltpu.VMEM((count, rows), jnp.bfloat16),
            pltpu.VMEM((planes, GROUP, STEPS, sensors), f32),
            pltpu.VMEM((GROUP, planes, STEPS, sensors), f32),
            pltpu.VMEM((planes, STEPS, sensors), f32),
            pltpu.VMEM((planes, STEPS, sensors), f32),
            dma((CHUNKS, GROUP)),
            dma((CHUNKS, GROUP)),
            dma((CHUNKS, planes)),
            dma((CHUNKS, planes)),
            dma((CHUNKS, planes)),
            dma((CHUNKS, planes)),
            dma((CHUNKS, GROUP)),
            dma((CHUNKS, GROUP)),
            dma((GROUP,)),
            dma((GROUP,)),
            dma,
            dma((CHIPS,)),
            dma((CHIPS,)),
            dma((CHIPS,)),
            dma((CHIPS,)),
            dma((GROUP,)),
            dma((GROUP,)),
            dma((planes,)),
            dma((planes,)),
        ],
        compiler_params=pltpu.CompilerParams(
            collective_id=0, has_side_effects=True, vmem_limit_bytes=56 * 1024 * 1024
        ),
        cost_estimate=pl.CostEstimate(
            flops=2 * rows * sources * count, bytes_accessed=4 * rows * sources, transcendentals=0
        ),
    )(
        connectome,
        history,
        delays,
        cycle_head,
        outside_afferent,
        init_state,
        lead_field,
    )


def solution(mesh):
    in_specs = (
        P("tgt", "src"),
        P("tgt", None, "src"),
        P("tgt", "src"),
        P(),
        P(),
        P(None, None, "tgt"),
        P("tgt", None),
    )
    out_specs = (P("tgt", None, None), P(None, None, ("tgt", "src")))
    devices = mesh.shape["tgt"]
    chosen = body
    if mesh.shape["src"] == 1 and devices % GROUP == 0 and devices >= 4 * GROUP:
        chosen = functools.partial(fused_body, devices // GROUP)
    return jax.shard_map(chosen, mesh=mesh, in_specs=in_specs, out_specs=out_specs, check_vma=False)
```

```python
import functools

import jax
import jax.numpy as jnp
from jax import lax
from jax.experimental import pallas as pl
from jax.experimental.pallas import tpu as pltpu
from jax.sharding import PartitionSpec as P

STEPS = 16
MESH = pl.DeviceIdType.MESH
GROUP = 8
CHIPS = GROUP // 2
CUTS = (0.2, 0.44, 0.68, 0.88, 1.0)
CHUNKS = len(CUTS)


def chunk_starts(blocks):
    return [0] + [2 * round(cut * blocks / 2) for cut in CUTS[:-1]] + [blocks]


integrator_step_width = 0.1
positive_synaptic_amplitude = 0.0325
negative_synaptic_amplitude = 0.11
interneuron_fraction = 0.5
global_link_scale = 30.0
stellate_contact_count = 135.0
recurrent_loop_contacts = 108.0
interneuron_contact_count = 33.75
peak_spike_rate = 5.0
logistic_slope_factor = 0.56
logistic_midpoint = 6.0


def spike_rate_response(cell_depolarization):
    return peak_spike_rate * jax.nn.sigmoid(
        logistic_slope_factor * (cell_depolarization - logistic_midpoint)
    )


def advance(carry, applied_stimulus, outside_afferent):
    (
        principal_cell_depolarization,
        stellate_mean_depolarization,
        interneuron_mean_depolarization,
        principal_cell_slope,
        excite_rate,
        interneuron_slope,
    ) = carry
    next_principal_cell_slope = principal_cell_slope + integrator_step_width * (
        positive_synaptic_amplitude
        * spike_rate_response(stellate_mean_depolarization - interneuron_mean_depolarization)
        - 2.0 * principal_cell_slope
        - principal_cell_depolarization
    )
    summed_afferent_rate = (
        outside_afferent
        + recurrent_loop_contacts
        * spike_rate_response(stellate_contact_count * principal_cell_depolarization)
        + global_link_scale * applied_stimulus
    )
    new_excite_rate = excite_rate + integrator_step_width * (
        positive_synaptic_amplitude * summed_afferent_rate
        - 2.0 * excite_rate
        - stellate_mean_depolarization
    )
    next_interneuron_slope = interneuron_slope + integrator_step_width * (
        negative_synaptic_amplitude
        * interneuron_contact_count
        * spike_rate_response(interneuron_contact_count * principal_cell_depolarization)
        - 2.0 * interneuron_fraction * interneuron_slope
        - interneuron_fraction * interneuron_fraction * interneuron_mean_depolarization
    )
    return (
        principal_cell_depolarization + integrator_step_width * principal_cell_slope,
        stellate_mean_depolarization + integrator_step_width * excite_rate,
        interneuron_mean_depolarization + integrator_step_width * interneuron_slope,
        next_principal_cell_slope,
        new_excite_rate,
        next_interneuron_slope,
    )


def integrate(init_state, outside_afferent, coupling):

    def one_step(carry, applied_stimulus):
        fresh = advance(carry, applied_stimulus, outside_afferent[:, None])
        return (fresh, fresh[1] - fresh[2])

    begin = tuple((init_state[member] for member in range(6)))
    final, potentials = lax.scan(one_step, begin, coupling)
    return (jnp.stack(final), potentials)


def body(connectome, history, delays, cycle_head, outside_afferent, init_state, lead_field):
    tgt_rows = connectome.shape[0]
    target_blocks = delays.shape[0]
    source_blocks = delays.shape[1]
    block_rows = tgt_rows // target_blocks
    block_cols = connectome.shape[1] // source_blocks
    members = history.shape[1]
    slots_all = history.shape[0] * lax.axis_size("tgt")
    tiles = connectome.reshape(target_blocks, block_rows, source_blocks, block_cols)
    moments = jnp.arange(STEPS, dtype=jnp.int32)
    lag_slot = (cycle_head[0] + moments[None, None, :] - delays[:, :, None]) % slots_all
    whole = lax.all_gather(history, "tgt", axis=0, tiled=True)
    stacked = whole.reshape(slots_all, members, source_blocks, block_cols)
    slot_ids = jnp.arange(slots_all, dtype=jnp.int32)
    wanted = lag_slot[0].T
    picker = (wanted[:, None, :] == slot_ids[None, :, None]).astype(jnp.bfloat16)
    window = jnp.einsum(
        "tkb,kmbs->tmbs", picker, stacked, preferred_element_type=jnp.float32
    ).astype(jnp.bfloat16)
    pieces = jnp.einsum("rbs,tmbs->tmr", tiles[0], window, preferred_element_type=jnp.float32)
    share = tgt_rows // lax.axis_size("src")
    offset_rows = lax.axis_index("src") * share
    summed = lax.psum(pieces, "src")
    final_full, potentials = integrate(init_state, outside_afferent, summed)
    final_state = lax.dynamic_slice_in_dim(final_full, offset_rows, share, 2)
    potential = potentials.astype(jnp.bfloat16)
    signal = lax.psum_scatter(
        jnp.einsum("tmr,rs->mts", potential, lead_field, preferred_element_type=jnp.float32),
        "tgt",
        scatter_dimension=0,
        tiled=True,
    )
    return (signal, final_state)


def fused_kernel(
    planes,
    conn_ref,
    hist_ref,
    delay_ref,
    head_ref,
    outside_ref,
    init_ref,
    lead_ref,
    signal_ref,
    final_ref,
    *scratch,
):
    held = scratch[:CHUNKS]
    tiles = scratch[CHUNKS : 2 * CHUNKS]
    (
        delay_vmem,
        delay_smem,
        acc,
        pair,
        parts,
        coupling,
        pot,
        eeg,
        eeg_plane,
        eeg_sum,
        eeg_line,
        piece_send,
        piece_recv,
        up_send,
        up_recv,
        down_send,
        down_recv,
        tile_send,
        tile_recv,
        delay_send,
        delay_recv,
        delay_local,
        pair_send,
        pair_recv,
        part_send,
        part_recv,
        plane_send,
        plane_recv,
        line_send,
        line_recv,
    ) = scratch[2 * CHUNKS :]
    me = lax.axis_index("tgt")
    z = me // GROUP
    p = me % GROUP
    core = p % 2
    chip = p // 2
    is_end = (z == 0) | (z == planes - 1)
    is_inner = (z > 0) & (z < planes - 1)
    rows = conn_ref.shape[0]
    members = hist_ref.shape[1]
    share = conn_ref.shape[1] // GROUP
    blocks = delay_ref.shape[1] // GROUP
    block_cols = share // blocks
    starts = chunk_starts(blocks)

    def peer(off):
        return lax.rem(p + off, GROUP)

    def line(off):
        return lax.rem(z + off, planes)

    def device(plane, place):
        return {"tgt": plane * GROUP + place}

    barrier = pltpu.get_barrier_semaphore()
    for off in range(1, GROUP):
        pl.semaphore_signal(barrier, inc=1, device_id=device(z, peer(off)), device_id_type=MESH)
    for off in range(1, planes):
        pl.semaphore_signal(barrier, inc=1, device_id=device(line(off), p), device_id_type=MESH)
    pl.semaphore_wait(barrier, GROUP + planes - 2)

    def remote(src, dst, send, recv, plane, place):
        return pltpu.make_async_remote_copy(
            src_ref=src, dst_ref=dst, send_sem=send, recv_sem=recv,
            device_id=device(plane, place), device_id_type=MESH,
        )

    def columns(place, c):
        width = (starts[c + 1] - starts[c]) * block_cols
        return pl.ds(pl.multiple_of(place * share + starts[c] * block_cols, 128), width)

    def piece_copy(c, off):
        return remote(
            hist_ref.at[0, :, columns(peer(off), c)], held[c].at[me],
            piece_send.at[c, off], piece_recv.at[c, p], z, peer(off),
        )

    def own_piece(c):
        return pltpu.make_async_copy(
            hist_ref.at[0, :, columns(p, c)], held[c].at[me], piece_recv.at[c, p]
        )

    def piece_arrival(c, off):
        slot = z * GROUP + peer(off)
        return remote(
            held[c].at[slot], held[c].at[slot],
            piece_send.at[c, off], piece_recv.at[c, peer(off)], z, peer(off),
        )

    def tile_copy(c, off):
        return remote(
            conn_ref.at[:, columns(peer(off), c)], tiles[c].at[p],
            tile_send.at[c, off], tile_recv.at[c, p], z, peer(off),
        )

    def own_tile(c):
        return pltpu.make_async_copy(
            conn_ref.at[:, columns(p, c)], tiles[c].at[p], tile_recv.at[c, p]
        )

    def tile_arrival(c, off):
        return remote(
            tiles[c].at[peer(off)], tiles[c].at[peer(off)],
            tile_send.at[c, off], tile_recv.at[c, peer(off)], z, peer(off),
        )

    def delay_copy(off):
        return remote(
            delay_ref, delay_vmem.at[p], delay_send.at[off], delay_recv.at[p], z, peer(off)
        )

    def delay_arrival(off):
        return remote(
            delay_ref, delay_vmem.at[peer(off)],
            delay_send.at[off], delay_recv.at[peer(off)], z, peer(off),
        )

    def plane_rows(plane):
        return pl.ds(plane * GROUP, GROUP)

    def up_copy(c, k):
        span = held[c].at[plane_rows(z - k)]
        return remote(span, span, up_send.at[c, k], up_recv.at[c, k], z + 1, p)

    def up_arrival(c, k):
        span = held[c].at[plane_rows(z - 1 - k)]
        return remote(span, span, up_send.at[c, k], up_recv.at[c, k], z - 1, p)

    def down_copy(c, k):
        span = held[c].at[plane_rows(z + k)]
        return remote(span, span, down_send.at[c, k], down_recv.at[c, k], z - 1, p)

    def down_arrival(c, k):
        span = held[c].at[plane_rows(z + 1 + k)]
        return remote(span, span, down_send.at[c, k], down_recv.at[c, k], z + 1, p)

    def sends_up(k):
        return (z + 1 < planes) & (z - k >= 0)

    def sends_down(k):
        return (z - 1 >= 0) & (z + k < planes)

    def send_pieces(c):
        own_piece(c).start()
        for off in range(1, GROUP):
            piece_copy(c, off).start()

    def send_tiles(c):
        own_tile(c).start()
        for off in range(1, GROUP):
            tile_copy(c, off).start()

    def forward(c, k):
        @pl.when(sends_up(k))
        def _():
            up_copy(c, k).start()

        @pl.when(sends_down(k))
        def _():
            down_copy(c, k).start()

    def line_arrives(c, k, here):
        @pl.when((z - 1 - k >= 0) & here)
        def _():
            up_arrival(c, k).wait_recv()

        @pl.when((z + 1 + k < planes) & here)
        def _():
            down_arrival(c, k).wait_recv()

    def line_stage(c, k):
        line_arrives(c, k, is_inner)
        if k + 2 < planes:
            forward(c, k + 1)

    def plane_stage(c):
        own_piece(c).wait()
        for off in range(1, GROUP):
            piece_arrival(c, off).wait_recv()
        forward(c, 0)

    head = head_ref[0]

    slots = planes * GROUP

    def slot_of(at):
        return at & (slots - 1) if slots & (slots - 1) == 0 else lax.rem(at, slots)

    def add_product(c, a):
        count = starts[c + 1] - starts[c]
        half = STEPS // 2
        for early in range(0, STEPS, half):
            total = None
            for first in range(0, count, 2):
                last = min(first + 2, count)
                spans = []
                for b in range(first, last):
                    base = head + 2 * slots - delay_smem[a, 0, p * blocks + starts[c] + b]
                    spans.append(
                        jnp.concatenate(
                            [
                                held[c][
                                    slot_of(base + t), :, b * block_cols : (b + 1) * block_cols
                                ]
                                for t in range(early, early + half)
                            ],
                            axis=0,
                        )
                    )
                term = lax.dot_general(
                    jnp.concatenate(spans, axis=1),
                    tiles[c][a, :, first * block_cols : last * block_cols],
                    (((1,), (1,)), ((), ())),
                    preferred_element_type=jnp.float32,
                )
                total = term if total is None else total + term
            acc[a, early * members : (early + half) * members, :] += total

    class Sum:
        def __init__(self, own, pair, parts, pair_send, pair_recv, part_send, part_recv):
            self.own, self.pair, self.parts = own, pair, parts
            self.pair_send, self.pair_recv = pair_send, pair_recv
            self.part_send, self.part_recv = part_send, part_recv

        def pair_copy(self, j):
            return remote(
                self.own.at[2 * j + 1 - core], self.pair.at[j],
                self.pair_send.at[j], self.pair_recv.at[j], z, 2 * chip + 1 - core,
            )

        def part_copy(self, off):
            j = lax.rem(chip + off, CHIPS)
            return remote(
                self.own.at[2 * j + core], self.parts.at[chip],
                self.part_send.at[off], self.part_recv.at[chip], z, 2 * j + core,
            )

        def part_arrival(self, off):
            j = lax.rem(chip + off, CHIPS)
            return remote(
                self.own.at[2 * j + core], self.parts.at[j],
                self.part_send.at[off], self.part_recv.at[j], z, 2 * j + core,
            )

        def pass_on(self, off):
            j = lax.rem(chip + off, CHIPS)
            self.pair_copy(j).wait_recv()
            self.own[2 * j + core] += self.pair[j]
            if off > 0:
                self.part_copy(off).start()

        def send(self, fill):
            order = list(range(1, CHIPS)) + [0]
            for at, off in enumerate(order):
                j = lax.rem(chip + off, CHIPS)
                fill(2 * j + 1 - core)
                self.pair_copy(j).start()
                fill(2 * j + core)
                if at > 0:
                    self.pass_on(order[at - 1])
            self.pass_on(order[-1])

        def total(self):
            value = self.own[2 * chip + core]
            for off in range(1, CHIPS):
                self.part_arrival(off).wait_recv()
                value = value + self.parts[lax.rem(chip + off, CHIPS)]
            return value

        def finish(self):
            for j in range(CHIPS):
                self.pair_copy(j).wait_send()
            for off in range(1, CHIPS):
                self.part_copy(off).wait_send()

    main = Sum(acc, pair, parts, pair_send, pair_recv, part_send, part_recv)
    def tiles_arrive(c):
        own_tile(c).wait()
        for off in range(1, GROUP):
            tile_arrival(c, off).wait_recv()

    def compute(c):
        tiles_arrive(c)
        for k in range(planes - 1):
            line_arrives(c, k, is_end)

        def one(a):
            add_product(c, a)

        if c < CHUNKS - 1:
            lax.fori_loop(0, GROUP, lambda a, carry: (one(a), carry)[1], 0)
        else:
            main.send(one)

    for off in range(1, GROUP):
        delay_copy(off).start()
    own_delay = pltpu.make_async_copy(delay_ref, delay_vmem.at[p], delay_recv.at[p])
    own_delay.start()
    for c in range(3):
        send_pieces(c)
    send_tiles(0)
    send_tiles(1)
    acc[...] = jnp.zeros_like(acc)
    for s in range(CHUNKS + planes - 1):
        if s == 0:
            plane_stage(0)
        if s + 3 < CHUNKS:
            send_pieces(s + 3)
        if s + 2 < CHUNKS:
            send_tiles(s + 2)
        if s + 1 < CHUNKS:
            plane_stage(s + 1)
        if s == 0:
            own_delay.wait()
            for off in range(1, GROUP):
                delay_arrival(off).wait_recv()
            table = pltpu.make_async_copy(delay_vmem, delay_smem, delay_local)
            table.start()
            table.wait()
        for k in range(planes - 1):
            if 0 <= s - 1 - k < CHUNKS:
                line_stage(s - 1 - k, k)
        if 0 <= s - planes + 1 < CHUNKS:
            compute(s - planes + 1)

    coupling[...] = main.total()

    state = tuple(init_ref[i] for i in range(6))
    member = lax.broadcasted_iota(jnp.int32, (members, rows), 0)
    outside = jnp.zeros((members, rows), jnp.float32)
    for m in range(members):
        outside = jnp.where(member == m, outside_ref[m], outside)
    for t in range(STEPS):
        stimulus = coupling[t * members : (t + 1) * members, :]
        state = advance(state, stimulus, outside)
        pot[t * members : (t + 1) * members, :] = (state[1] - state[2]).astype(jnp.bfloat16)
    for i in range(6):
        final_ref[i] = state[i]

    count = STEPS * members
    row = lax.broadcasted_iota(jnp.int32, (count, count), 0)
    col = lax.broadcasted_iota(jnp.int32, (count, count), 1)
    order = jnp.where(col == (row % STEPS) * members + row // STEPS, 1.0, 0.0).astype(jnp.bfloat16)
    ordered = jnp.dot(order, pot[...], preferred_element_type=jnp.float32).astype(jnp.bfloat16)
    sensors = lead_ref.shape[1]
    eeg[...] = jnp.dot(ordered, lead_ref[...], preferred_element_type=jnp.float32).reshape(
        planes, GROUP, STEPS, sensors
    )

    def plane_copy(off):
        return remote(
            eeg.at[:, peer(off)], eeg_plane.at[p], plane_send.at[off], plane_recv.at[p], z, peer(off)
        )

    def plane_arrival(off):
        return remote(
            eeg.at[:, peer(off)], eeg_plane.at[peer(off)],
            plane_send.at[off], plane_recv.at[peer(off)], z, peer(off),
        )

    for off in range(1, GROUP):
        plane_copy(off).start()
    eeg_plane[p] = eeg[:, p]
    for off in range(1, GROUP):
        plane_arrival(off).wait_recv()
    over_plane = eeg_plane[0]
    for q in range(1, GROUP):
        over_plane = over_plane + eeg_plane[q]
    eeg_sum[...] = over_plane

    def line_copy(off):
        return remote(
            eeg_sum.at[line(off)], eeg_line.at[z], line_send.at[off], line_recv.at[z], line(off), p
        )

    def line_arrival(off):
        return remote(
            eeg_sum.at[line(off)], eeg_line.at[line(off)],
            line_send.at[off], line_recv.at[line(off)], line(off), p,
        )

    for off in range(1, planes):
        line_copy(off).start()
    eeg_line[z] = eeg_sum[z]
    for off in range(1, planes):
        line_arrival(off).wait_recv()
    over_line = eeg_line[0]
    for q in range(1, planes):
        over_line = over_line + eeg_line[q]
    signal_ref[0] = over_line

    for off in range(1, GROUP):
        delay_copy(off).wait_send()
        plane_copy(off).wait_send()
    main.finish()

    for off in range(1, planes):
        line_copy(off).wait_send()
    for c in range(CHUNKS):
        for off in range(1, GROUP):
            piece_copy(c, off).wait_send()
            tile_copy(c, off).wait_send()
        for k in range(planes - 1):
            @pl.when(sends_up(k))
            def _(c=c, k=k):
                up_copy(c, k).wait_send()

            @pl.when(sends_down(k))
            def _(c=c, k=k):
                down_copy(c, k).wait_send()


def fused_body(planes, connectome, history, delays, cycle_head, outside_afferent, init_state, lead_field):
    rows, sources = connectome.shape
    members = history.shape[1]
    sensors = lead_field.shape[1]
    slots = planes * GROUP
    share = sources // GROUP
    blocks = delays.shape[1] // GROUP
    starts = chunk_starts(blocks)
    widths = [(stop - start) * (share // blocks) for start, stop in zip(starts, starts[1:])]
    count = STEPS * members
    dma = pltpu.SemaphoreType.DMA
    f32 = jnp.float32
    vmem = pl.BlockSpec(memory_space=pltpu.VMEM)
    smem = pl.BlockSpec(memory_space=pltpu.SMEM)
    hbm = pl.BlockSpec(memory_space=pl.ANY)
    return pl.pallas_call(
        functools.partial(fused_kernel, planes),
        out_shape=(
            jax.ShapeDtypeStruct((1, STEPS, sensors), f32),
            jax.ShapeDtypeStruct(init_state.shape, f32),
        ),
        in_specs=[hbm, hbm, hbm, smem, smem, vmem, vmem],
        out_specs=(vmem, vmem),
        scratch_shapes=[pltpu.VMEM((slots, members, width), jnp.bfloat16) for width in widths]
        + [pltpu.VMEM((GROUP, rows, width), jnp.bfloat16) for width in widths]
        + [
            pltpu.VMEM((GROUP, 1, delays.shape[1]), jnp.int32),
            pltpu.SMEM((GROUP, 1, delays.shape[1]), jnp.int32),
            pltpu.VMEM((GROUP, count, rows), f32),
            pltpu.VMEM((CHIPS, count, rows), f32),
            pltpu.VMEM((CHIPS, count, rows), f32),
            pltpu.VMEM((count, rows), f32),
            pltpu.VMEM((count, rows), jnp.bfloat16),
            pltpu.VMEM((planes, GROUP, STEPS, sensors), f32),
            pltpu.VMEM((GROUP, planes, STEPS, sensors), f32),
            pltpu.VMEM((planes, STEPS, sensors), f32),
            pltpu.VMEM((planes, STEPS, sensors), f32),
            dma((CHUNKS, GROUP)),
            dma((CHUNKS, GROUP)),
            dma((CHUNKS, planes)),
            dma((CHUNKS, planes)),
            dma((CHUNKS, planes)),
            dma((CHUNKS, planes)),
            dma((CHUNKS, GROUP)),
            dma((CHUNKS, GROUP)),
            dma((GROUP,)),
            dma((GROUP,)),
            dma,
            dma((CHIPS,)),
            dma((CHIPS,)),
            dma((CHIPS,)),
            dma((CHIPS,)),
            dma((GROUP,)),
            dma((GROUP,)),
            dma((planes,)),
            dma((planes,)),
        ],
        compiler_params=pltpu.CompilerParams(
            collective_id=0, has_side_effects=True, vmem_limit_bytes=56 * 1024 * 1024
        ),
        cost_estimate=pl.CostEstimate(
            flops=2 * rows * sources * count, bytes_accessed=4 * rows * sources, transcendentals=0
        ),
    )(
        connectome,
        history,
        delays,
        cycle_head,
        outside_afferent,
        init_state,
        lead_field,
    )


def solution(mesh):
    in_specs = (
        P("tgt", "src"),
        P("tgt", None, "src"),
        P("tgt", "src"),
        P(),
        P(),
        P(None, None, "tgt"),
        P("tgt", None),
    )
    out_specs = (P("tgt", None, None), P(None, None, ("tgt", "src")))
    devices = mesh.shape["tgt"]
    chosen = body
    if mesh.shape["src"] == 1 and devices % GROUP == 0 and devices >= 4 * GROUP:
        chosen = functools.partial(fused_body, devices // GROUP)
    return jax.shard_map(chosen, mesh=mesh, in_specs=in_specs, out_specs=out_specs, check_vma=False)
```

```python
import functools

import jax
import jax.numpy as jnp
from jax import lax
from jax.experimental import pallas as pl
from jax.experimental.pallas import tpu as pltpu
from jax.sharding import PartitionSpec as P

STEPS = 16
MESH = pl.DeviceIdType.MESH
GROUP = 8
CHIPS = GROUP // 2
CUTS = (0.2, 0.44, 0.68, 0.88, 1.0)
CHUNKS = len(CUTS)


def chunk_starts(blocks):
    return [0] + [2 * round(cut * blocks / 2) for cut in CUTS[:-1]] + [blocks]


integrator_step_width = 0.1
positive_synaptic_amplitude = 0.0325
negative_synaptic_amplitude = 0.11
interneuron_fraction = 0.5
global_link_scale = 30.0
stellate_contact_count = 135.0
recurrent_loop_contacts = 108.0
interneuron_contact_count = 33.75
peak_spike_rate = 5.0
logistic_slope_factor = 0.56
logistic_midpoint = 6.0


def spike_rate_response(cell_depolarization):
    return peak_spike_rate * jax.nn.sigmoid(
        logistic_slope_factor * (cell_depolarization - logistic_midpoint)
    )


def advance(carry, applied_stimulus, outside_afferent):
    (
        principal_cell_depolarization,
        stellate_mean_depolarization,
        interneuron_mean_depolarization,
        principal_cell_slope,
        excite_rate,
        interneuron_slope,
    ) = carry
    next_principal_cell_slope = principal_cell_slope + integrator_step_width * (
        positive_synaptic_amplitude
        * spike_rate_response(stellate_mean_depolarization - interneuron_mean_depolarization)
        - 2.0 * principal_cell_slope
        - principal_cell_depolarization
    )
    summed_afferent_rate = (
        outside_afferent
        + recurrent_loop_contacts
        * spike_rate_response(stellate_contact_count * principal_cell_depolarization)
        + global_link_scale * applied_stimulus
    )
    new_excite_rate = excite_rate + integrator_step_width * (
        positive_synaptic_amplitude * summed_afferent_rate
        - 2.0 * excite_rate
        - stellate_mean_depolarization
    )
    next_interneuron_slope = interneuron_slope + integrator_step_width * (
        negative_synaptic_amplitude
        * interneuron_contact_count
        * spike_rate_response(interneuron_contact_count * principal_cell_depolarization)
        - 2.0 * interneuron_fraction * interneuron_slope
        - interneuron_fraction * interneuron_fraction * interneuron_mean_depolarization
    )
    return (
        principal_cell_depolarization + integrator_step_width * principal_cell_slope,
        stellate_mean_depolarization + integrator_step_width * excite_rate,
        interneuron_mean_depolarization + integrator_step_width * interneuron_slope,
        next_principal_cell_slope,
        new_excite_rate,
        next_interneuron_slope,
    )


def integrate(init_state, outside_afferent, coupling):

    def one_step(carry, applied_stimulus):
        fresh = advance(carry, applied_stimulus, outside_afferent[:, None])
        return (fresh, fresh[1] - fresh[2])

    begin = tuple((init_state[member] for member in range(6)))
    final, potentials = lax.scan(one_step, begin, coupling)
    return (jnp.stack(final), potentials)


def body(connectome, history, delays, cycle_head, outside_afferent, init_state, lead_field):
    tgt_rows = connectome.shape[0]
    target_blocks = delays.shape[0]
    source_blocks = delays.shape[1]
    block_rows = tgt_rows // target_blocks
    block_cols = connectome.shape[1] // source_blocks
    members = history.shape[1]
    slots_all = history.shape[0] * lax.axis_size("tgt")
    tiles = connectome.reshape(target_blocks, block_rows, source_blocks, block_cols)
    moments = jnp.arange(STEPS, dtype=jnp.int32)
    lag_slot = (cycle_head[0] + moments[None, None, :] - delays[:, :, None]) % slots_all
    whole = lax.all_gather(history, "tgt", axis=0, tiled=True)
    stacked = whole.reshape(slots_all, members, source_blocks, block_cols)
    slot_ids = jnp.arange(slots_all, dtype=jnp.int32)
    wanted = lag_slot[0].T
    picker = (wanted[:, None, :] == slot_ids[None, :, None]).astype(jnp.bfloat16)
    window = jnp.einsum(
        "tkb,kmbs->tmbs", picker, stacked, preferred_element_type=jnp.float32
    ).astype(jnp.bfloat16)
    pieces = jnp.einsum("rbs,tmbs->tmr", tiles[0], window, preferred_element_type=jnp.float32)
    share = tgt_rows // lax.axis_size("src")
    offset_rows = lax.axis_index("src") * share
    summed = lax.psum(pieces, "src")
    final_full, potentials = integrate(init_state, outside_afferent, summed)
    final_state = lax.dynamic_slice_in_dim(final_full, offset_rows, share, 2)
    potential = potentials.astype(jnp.bfloat16)
    signal = lax.psum_scatter(
        jnp.einsum("tmr,rs->mts", potential, lead_field, preferred_element_type=jnp.float32),
        "tgt",
        scatter_dimension=0,
        tiled=True,
    )
    return (signal, final_state)


def fused_kernel(
    planes,
    conn_ref,
    hist_ref,
    delay_ref,
    head_ref,
    outside_ref,
    init_ref,
    lead_ref,
    signal_ref,
    final_ref,
    *scratch,
):
    held = scratch[:CHUNKS]
    tiles = scratch[CHUNKS : 2 * CHUNKS]
    (
        delay_vmem,
        delay_smem,
        acc,
        pair,
        parts,
        coupling,
        pot,
        eeg,
        eeg_plane,
        eeg_sum,
        eeg_line,
        piece_send,
        piece_recv,
        up_send,
        up_recv,
        down_send,
        down_recv,
        tile_send,
        tile_recv,
        delay_send,
        delay_recv,
        delay_local,
        pair_send,
        pair_recv,
        part_send,
        part_recv,
        plane_send,
        plane_recv,
        line_send,
        line_recv,
    ) = scratch[2 * CHUNKS :]
    me = lax.axis_index("tgt")
    z = me // GROUP
    p = me % GROUP
    core = p % 2
    chip = p // 2
    is_end = (z == 0) | (z == planes - 1)
    is_inner = (z > 0) & (z < planes - 1)
    rows = conn_ref.shape[0]
    members = hist_ref.shape[1]
    share = conn_ref.shape[1] // GROUP
    blocks = delay_ref.shape[1] // GROUP
    block_cols = share // blocks
    starts = chunk_starts(blocks)

    def peer(off):
        return lax.rem(p + off, GROUP)

    def line(off):
        return lax.rem(z + off, planes)

    def device(plane, place):
        return {"tgt": plane * GROUP + place}

    barrier = pltpu.get_barrier_semaphore()
    for off in range(1, GROUP):
        pl.semaphore_signal(barrier, inc=1, device_id=device(z, peer(off)), device_id_type=MESH)
    for off in range(1, planes):
        pl.semaphore_signal(barrier, inc=1, device_id=device(line(off), p), device_id_type=MESH)
    pl.semaphore_wait(barrier, GROUP + planes - 2)

    def remote(src, dst, send, recv, plane, place):
        return pltpu.make_async_remote_copy(
            src_ref=src, dst_ref=dst, send_sem=send, recv_sem=recv,
            device_id=device(plane, place), device_id_type=MESH,
        )

    def columns(place, c):
        width = (starts[c + 1] - starts[c]) * block_cols
        return pl.ds(pl.multiple_of(place * share + starts[c] * block_cols, 128), width)

    def piece_copy(c, off):
        return remote(
            hist_ref.at[0, :, columns(peer(off), c)], held[c].at[me],
            piece_send.at[c, off], piece_recv.at[c, p], z, peer(off),
        )

    def own_piece(c):
        return pltpu.make_async_copy(
            hist_ref.at[0, :, columns(p, c)], held[c].at[me], piece_recv.at[c, p]
        )

    def piece_arrival(c, off):
        slot = z * GROUP + peer(off)
        return remote(
            held[c].at[slot], held[c].at[slot],
            piece_send.at[c, off], piece_recv.at[c, peer(off)], z, peer(off),
        )

    def tile_copy(c, off):
        return remote(
            conn_ref.at[:, columns(peer(off), c)], tiles[c].at[p],
            tile_send.at[c, off], tile_recv.at[c, p], z, peer(off),
        )

    def own_tile(c):
        return pltpu.make_async_copy(
            conn_ref.at[:, columns(p, c)], tiles[c].at[p], tile_recv.at[c, p]
        )

    def tile_arrival(c, off):
        return remote(
            tiles[c].at[peer(off)], tiles[c].at[peer(off)],
            tile_send.at[c, off], tile_recv.at[c, peer(off)], z, peer(off),
        )

    def delay_copy(off):
        return remote(
            delay_ref, delay_vmem.at[p], delay_send.at[off], delay_recv.at[p], z, peer(off)
        )

    def delay_arrival(off):
        return remote(
            delay_ref, delay_vmem.at[peer(off)],
            delay_send.at[off], delay_recv.at[peer(off)], z, peer(off),
        )

    def plane_rows(plane):
        return pl.ds(plane * GROUP, GROUP)

    def up_copy(c, k):
        span = held[c].at[plane_rows(z - k)]
        return remote(span, span, up_send.at[c, k], up_recv.at[c, k], z + 1, p)

    def up_arrival(c, k):
        span = held[c].at[plane_rows(z - 1 - k)]
        return remote(span, span, up_send.at[c, k], up_recv.at[c, k], z - 1, p)

    def down_copy(c, k):
        span = held[c].at[plane_rows(z + k)]
        return remote(span, span, down_send.at[c, k], down_recv.at[c, k], z - 1, p)

    def down_arrival(c, k):
        span = held[c].at[plane_rows(z + 1 + k)]
        return remote(span, span, down_send.at[c, k], down_recv.at[c, k], z + 1, p)

    def sends_up(k):
        return (z + 1 < planes) & (z - k >= 0)

    def sends_down(k):
        return (z - 1 >= 0) & (z + k < planes)

    def send_pieces(c):
        own_piece(c).start()
        for off in range(1, GROUP):
            piece_copy(c, off).start()

    def send_tiles(c):
        own_tile(c).start()
        for off in range(1, GROUP):
            tile_copy(c, off).start()

    def forward(c, k):
        @pl.when(sends_up(k))
        def _():
            up_copy(c, k).start()

        @pl.when(sends_down(k))
        def _():
            down_copy(c, k).start()

    def line_arrives(c, k, here):
        @pl.when((z - 1 - k >= 0) & here)
        def _():
            up_arrival(c, k).wait_recv()

        @pl.when((z + 1 + k < planes) & here)
        def _():
            down_arrival(c, k).wait_recv()

    def line_stage(c, k):
        line_arrives(c, k, is_inner)
        if k + 2 < planes:
            forward(c, k + 1)

    def plane_stage(c):
        own_piece(c).wait()
        for off in range(1, GROUP):
            piece_arrival(c, off).wait_recv()
        forward(c, 0)

    head = head_ref[0]

    slots = planes * GROUP

    def slot_of(at):
        return at & (slots - 1) if slots & (slots - 1) == 0 else lax.rem(at, slots)

    def product(c, a, tile, table):
        total = None
        count = starts[c + 1] - starts[c]
        for first in range(0, count, 2):
            last = min(first + 2, count)
            spans = []
            for b in range(first, last):
                base = head + 2 * slots - table[a, 0, p * blocks + starts[c] + b]
                spans.append(
                    jnp.concatenate(
                        [
                            held[c][
                                slot_of(base + t),
                                :,
                                b * block_cols : (b + 1) * block_cols,
                            ]
                            for t in range(STEPS)
                        ],
                        axis=0,
                    )
                )
            window = jnp.concatenate(spans, axis=1)
            term = lax.dot_general(
                window,
                tile[a, :, first * block_cols : last * block_cols],
                (((1,), (1,)), ((), ())),
                preferred_element_type=jnp.float32,
            )
            total = term if total is None else total + term
        return total

    class Sum:
        def __init__(self, own, pair, parts, pair_send, pair_recv, part_send, part_recv):
            self.own, self.pair, self.parts = own, pair, parts
            self.pair_send, self.pair_recv = pair_send, pair_recv
            self.part_send, self.part_recv = part_send, part_recv

        def pair_copy(self, j):
            return remote(
                self.own.at[2 * j + 1 - core], self.pair.at[j],
                self.pair_send.at[j], self.pair_recv.at[j], z, 2 * chip + 1 - core,
            )

        def part_copy(self, off):
            j = lax.rem(chip + off, CHIPS)
            return remote(
                self.own.at[2 * j + core], self.parts.at[chip],
                self.part_send.at[off], self.part_recv.at[chip], z, 2 * j + core,
            )

        def part_arrival(self, off):
            j = lax.rem(chip + off, CHIPS)
            return remote(
                self.own.at[2 * j + core], self.parts.at[j],
                self.part_send.at[off], self.part_recv.at[j], z, 2 * j + core,
            )

        def pass_on(self, off):
            j = lax.rem(chip + off, CHIPS)
            self.pair_copy(j).wait_recv()
            self.own[2 * j + core] += self.pair[j]
            if off > 0:
                self.part_copy(off).start()

        def send(self, fill):
            order = list(range(1, CHIPS)) + [0]
            for at, off in enumerate(order):
                j = lax.rem(chip + off, CHIPS)
                fill(2 * j + 1 - core)
                self.pair_copy(j).start()
                fill(2 * j + core)
                if at > 0:
                    self.pass_on(order[at - 1])
            self.pass_on(order[-1])

        def total(self):
            value = self.own[2 * chip + core]
            for off in range(1, CHIPS):
                self.part_arrival(off).wait_recv()
                value = value + self.parts[lax.rem(chip + off, CHIPS)]
            return value

        def finish(self):
            for j in range(CHIPS):
                self.pair_copy(j).wait_send()
            for off in range(1, CHIPS):
                self.part_copy(off).wait_send()

    main = Sum(acc, pair, parts, pair_send, pair_recv, part_send, part_recv)
    def tiles_arrive(c):
        own_tile(c).wait()
        for off in range(1, GROUP):
            tile_arrival(c, off).wait_recv()

    def compute(c):
        tiles_arrive(c)
        for k in range(planes - 1):
            line_arrives(c, k, is_end)

        def one(a):
            acc[a] += product(c, a, tiles[c], delay_smem)

        if c < CHUNKS - 1:
            lax.fori_loop(0, GROUP, lambda a, carry: (one(a), carry)[1], 0)
        else:
            main.send(one)

    for off in range(1, GROUP):
        delay_copy(off).start()
    own_delay = pltpu.make_async_copy(delay_ref, delay_vmem.at[p], delay_recv.at[p])
    own_delay.start()
    send_pieces(0)
    send_pieces(1)
    acc[...] = jnp.zeros_like(acc)
    for s in range(CHUNKS + planes - 1):
        if s < CHUNKS:
            plane_stage(s)
            if s + 2 < CHUNKS:
                send_pieces(s + 2)
            send_tiles(s)
        if s == 0:
            own_delay.wait()
            for off in range(1, GROUP):
                delay_arrival(off).wait_recv()
            table = pltpu.make_async_copy(delay_vmem, delay_smem, delay_local)
            table.start()
            table.wait()
        for k in range(planes - 1):
            if 0 <= s - 1 - k < CHUNKS:
                line_stage(s - 1 - k, k)
        if 0 <= s - planes + 1 < CHUNKS:
            compute(s - planes + 1)

    coupling[...] = main.total()

    state = tuple(init_ref[i] for i in range(6))
    member = lax.broadcasted_iota(jnp.int32, (members, rows), 0)
    outside = jnp.zeros((members, rows), jnp.float32)
    for m in range(members):
        outside = jnp.where(member == m, outside_ref[m], outside)
    for t in range(STEPS):
        stimulus = coupling[t * members : (t + 1) * members, :]
        state = advance(state, stimulus, outside)
        pot[t * members : (t + 1) * members, :] = (state[1] - state[2]).astype(jnp.bfloat16)
    for i in range(6):
        final_ref[i] = state[i]

    count = STEPS * members
    row = lax.broadcasted_iota(jnp.int32, (count, count), 0)
    col = lax.broadcasted_iota(jnp.int32, (count, count), 1)
    order = jnp.where(col == (row % STEPS) * members + row // STEPS, 1.0, 0.0).astype(jnp.bfloat16)
    ordered = jnp.dot(order, pot[...], preferred_element_type=jnp.float32).astype(jnp.bfloat16)
    sensors = lead_ref.shape[1]
    eeg[...] = jnp.dot(ordered, lead_ref[...], preferred_element_type=jnp.float32).reshape(
        planes, GROUP, STEPS, sensors
    )

    def plane_copy(off):
        return remote(
            eeg.at[:, peer(off)], eeg_plane.at[p], plane_send.at[off], plane_recv.at[p], z, peer(off)
        )

    def plane_arrival(off):
        return remote(
            eeg.at[:, peer(off)], eeg_plane.at[peer(off)],
            plane_send.at[off], plane_recv.at[peer(off)], z, peer(off),
        )

    for off in range(1, GROUP):
        plane_copy(off).start()
    eeg_plane[p] = eeg[:, p]
    for off in range(1, GROUP):
        plane_arrival(off).wait_recv()
    over_plane = eeg_plane[0]
    for q in range(1, GROUP):
        over_plane = over_plane + eeg_plane[q]
    eeg_sum[...] = over_plane

    def line_copy(off):
        return remote(
            eeg_sum.at[line(off)], eeg_line.at[z], line_send.at[off], line_recv.at[z], line(off), p
        )

    def line_arrival(off):
        return remote(
            eeg_sum.at[line(off)], eeg_line.at[line(off)],
            line_send.at[off], line_recv.at[line(off)], line(off), p,
        )

    for off in range(1, planes):
        line_copy(off).start()
    eeg_line[z] = eeg_sum[z]
    for off in range(1, planes):
        line_arrival(off).wait_recv()
    over_line = eeg_line[0]
    for q in range(1, planes):
        over_line = over_line + eeg_line[q]
    signal_ref[0] = over_line

    for off in range(1, GROUP):
        delay_copy(off).wait_send()
        plane_copy(off).wait_send()
    main.finish()

    for off in range(1, planes):
        line_copy(off).wait_send()
    for c in range(CHUNKS):
        for off in range(1, GROUP):
            piece_copy(c, off).wait_send()
            tile_copy(c, off).wait_send()
        for k in range(planes - 1):
            @pl.when(sends_up(k))
            def _(c=c, k=k):
                up_copy(c, k).wait_send()

            @pl.when(sends_down(k))
            def _(c=c, k=k):
                down_copy(c, k).wait_send()


def fused_body(planes, connectome, history, delays, cycle_head, outside_afferent, init_state, lead_field):
    rows, sources = connectome.shape
    members = history.shape[1]
    sensors = lead_field.shape[1]
    slots = planes * GROUP
    share = sources // GROUP
    blocks = delays.shape[1] // GROUP
    starts = chunk_starts(blocks)
    widths = [(stop - start) * (share // blocks) for start, stop in zip(starts, starts[1:])]
    count = STEPS * members
    dma = pltpu.SemaphoreType.DMA
    f32 = jnp.float32
    vmem = pl.BlockSpec(memory_space=pltpu.VMEM)
    smem = pl.BlockSpec(memory_space=pltpu.SMEM)
    hbm = pl.BlockSpec(memory_space=pl.ANY)
    return pl.pallas_call(
        functools.partial(fused_kernel, planes),
        out_shape=(
            jax.ShapeDtypeStruct((1, STEPS, sensors), f32),
            jax.ShapeDtypeStruct(init_state.shape, f32),
        ),
        in_specs=[hbm, hbm, hbm, smem, smem, vmem, vmem],
        out_specs=(vmem, vmem),
        scratch_shapes=[pltpu.VMEM((slots, members, width), jnp.bfloat16) for width in widths]
        + [pltpu.VMEM((GROUP, rows, width), jnp.bfloat16) for width in widths]
        + [
            pltpu.VMEM((GROUP, 1, delays.shape[1]), jnp.int32),
            pltpu.SMEM((GROUP, 1, delays.shape[1]), jnp.int32),
            pltpu.VMEM((GROUP, count, rows), f32),
            pltpu.VMEM((CHIPS, count, rows), f32),
            pltpu.VMEM((CHIPS, count, rows), f32),
            pltpu.VMEM((count, rows), f32),
            pltpu.VMEM((count, rows), jnp.bfloat16),
            pltpu.VMEM((planes, GROUP, STEPS, sensors), f32),
            pltpu.VMEM((GROUP, planes, STEPS, sensors), f32),
            pltpu.VMEM((planes, STEPS, sensors), f32),
            pltpu.VMEM((planes, STEPS, sensors), f32),
            dma((CHUNKS, GROUP)),
            dma((CHUNKS, GROUP)),
            dma((CHUNKS, planes)),
            dma((CHUNKS, planes)),
            dma((CHUNKS, planes)),
            dma((CHUNKS, planes)),
            dma((CHUNKS, GROUP)),
            dma((CHUNKS, GROUP)),
            dma((GROUP,)),
            dma((GROUP,)),
            dma,
            dma((CHIPS,)),
            dma((CHIPS,)),
            dma((CHIPS,)),
            dma((CHIPS,)),
            dma((GROUP,)),
            dma((GROUP,)),
            dma((planes,)),
            dma((planes,)),
        ],
        compiler_params=pltpu.CompilerParams(
            collective_id=0, has_side_effects=True, vmem_limit_bytes=56 * 1024 * 1024
        ),
        cost_estimate=pl.CostEstimate(
            flops=2 * rows * sources * count, bytes_accessed=4 * rows * sources, transcendentals=0
        ),
    )(
        connectome,
        history,
        delays,
        cycle_head,
        outside_afferent,
        init_state,
        lead_field,
    )


def solution(mesh):
    in_specs = (
        P("tgt", "src"),
        P("tgt", None, "src"),
        P("tgt", "src"),
        P(),
        P(),
        P(None, None, "tgt"),
        P("tgt", None),
    )
    out_specs = (P("tgt", None, None), P(None, None, ("tgt", "src")))
    devices = mesh.shape["tgt"]
    chosen = body
    if mesh.shape["src"] == 1 and devices % GROUP == 0 and devices >= 4 * GROUP:
        chosen = functools.partial(fused_body, devices // GROUP)
    return jax.shard_map(chosen, mesh=mesh, in_specs=in_specs, out_specs=out_specs, check_vma=False)
```
